32 devices in a mesh: groups: 2 (over y), pipe: 4 (over z), hour: 2 (over x), seg: 2 (over core).
Axes of the slice: x: 2, y: 2, z: 4, core: 2. Of those that a mesh axis runs over, the one named last changes fastest.
Arguments:
- segment_flow: float32 [16, 64, 1024], P(('groups', 'hour'), 'seg', 'pipe'), parts along dimension 0, may hold values from -4 to 4
- linepack: float32 [16, 64, 1024], P(('groups', 'hour'), 'seg', 'pipe'), parts along dimension 0, may hold values from 0.2 to 2.4
- mass_dual: float32 [16, 64, 1024], P(('groups', 'hour'), 'seg', 'pipe'), parts along dimension 0, may hold values from -3 to 3
- momentum_dual: float32 [16, 64, 1024], P(('groups', 'hour'), 'seg', 'pipe'), parts along dimension 0, may hold values from -3 to 3
- contract_dual: float32 [16, 2, 32, 128], P(('groups', 'hour'), 'seg', 'pipe'), parts along dimension 0, may hold values from -3 to 3
- flow_cost: float32 [16, 64, 1024], P(('groups', 'hour'), 'seg', 'pipe'), parts along dimension 0, may hold values from -24 to 24
- injection: float32 [16, 64, 1024], P(('groups', 'hour'), 'seg', 'pipe'), parts along dimension 0, may hold values from -3 to 3
- contract_target: float32 [16, 2, 32, 128], P(('groups', 'hour'), 'seg', 'pipe'), parts along dimension 0, may hold values from 0.4 to 2
- friction_table: float32 [16], replicated, may hold values from 0.3 to 3
- friction_class: int32 [64, 2048], P('seg', ('groups', 'pipe')), parts along dimension 1, may hold values from 0 to 15
- matching: int32 [2048], P('groups'), parts along dimension 0, may hold values from 0 to 1023, as said below
- contract_map: int32 [16, 1024], P(('groups', 'hour')), parts along dimension 0, may hold values from 0 to 127
Outputs:
- flow_final: float32 [16, 64, 1024], P(('groups', 'hour'), 'seg', 'pipe'), parts along dimension 0
- linepack_final: float32 [16, 64, 1024], P(('groups', 'hour'), 'seg', 'pipe'), parts along dimension 0
- mass_dual_final: float32 [16, 64, 1024], P(('groups', 'hour'), 'seg', 'pipe'), parts along dimension 0
- momentum_dual_final: float32 [16, 64, 1024], P(('groups', 'hour'), 'seg', 'pipe'), parts along dimension 0
- contract_dual_final: float32 [16, 2, 32, 128], P(('groups', 'hour'), 'seg', 'pipe'), parts along dimension 0
- primal_weight: float32 [2], P('groups'), parts along dimension 0
The draws below stay inside these ranges and needn't reach their ends.
There are 2 independent parts, one for each index of `groups`. The reference program is written for one: setup_inputs(seed, part) draws one part's arguments, and reference() takes and returns one part's arrays. A program takes and returns all parts, laid end to end along the dimension named above; an argument that names none is the same for every part. Nothing has to cross between parts.
Inputs may be any that keep to these rules, and one draw needn't show every extreme that they name: `matching`: every pipe's inlet is fed by the outlet of exactly one pipe: each number of 0 to 1023 appears once; for any two blocks of 256 consecutive pipes, exactly 64 pipes of the first are fed from outlets of the second.
All inputs are finite; a program needn't handle non-finite values.
Results may differ from the reference program's by a relative error of at most 0.0001.
Values sent between devices are 32-bit elements; how exact they have to be, the bound alone decides.
A program may use at most 64 MiB of HBM per device.

```python
import math
import jax
import jax.numpy as jnp

PIPE_DEV = 256
SEGS = 64
NC = 128
NCLS = 16
ITERS = 2
PIPES = 1024
HOURS = 8
SEG_PARTS = 2
SEG_BLOCK = 32


def draw_flow_cost(key, part):
    normal_key = jax.random.fold_in(jax.random.fold_in(key, 17), 0)
    pipe_rank = jnp.arange(PIPES, dtype=jnp.float32) / PIPES
    pipe_scale = 0.3 * 10.0 ** pipe_rank
    normal_part = jnp.clip(jax.random.normal(normal_key, (HOURS, SEGS, PIPES), jnp.float32), -4.0, 4.0)
    return normal_part * pipe_scale


def draw_matching(key, part):
    base_key = jax.random.fold_in(key, 29)
    block_count = PIPES // PIPE_DEV
    per_peer = PIPE_DEV // block_count
    dest_keys = jax.random.split(jax.random.fold_in(base_key, 1), block_count)
    source_keys = jax.random.split(jax.random.fold_in(base_key, 2), block_count)
    dest_order = jax.vmap(lambda one_key: jax.random.permutation(one_key, PIPE_DEV))(dest_keys).astype(jnp.int32)
    source_order = jax.vmap(lambda one_key: jax.random.permutation(one_key, PIPE_DEV))(source_keys).astype(jnp.int32)
    offsets = jax.random.permutation(jax.random.fold_in(base_key, 3), block_count).astype(jnp.int32)
    blocks = jnp.arange(block_count, dtype=jnp.int32)[:, None]
    group_index = dest_order // per_peer
    slot_index = dest_order % per_peer
    offset_used = jnp.take(offsets, group_index, axis=0)
    source_block = (blocks + offset_used) % block_count
    local_index = source_order[source_block, offset_used * per_peer + slot_index]
    return (source_block * PIPE_DEV + local_index).reshape(-1).astype(jnp.int32)


def place_ends(drawn, rng, least, high):
    longest = drawn.shape.index(max(drawn.shape))
    spots = []
    for shift in (0, 1):
        where = [jax.random.randint(jax.random.fold_in(rng, axis), (), 0, length) for axis, length in enumerate(drawn.shape)]
        where[longest] = (where[longest] + shift) % drawn.shape[longest]
        spots.append(tuple(where))
    return drawn.at[spots[0]].set(least).at[spots[1]].set(high)


def shard_levels(stream_key, shape, cuts, smallest, high):
    gain, own = 1.0, jax.random.fold_in(stream_key, 6)
    for position, shards_of in cuts:
        steps = jnp.exp(jax.random.uniform(jax.random.fold_in(own, position), (shards_of,), jnp.float32, smallest / len(cuts), high / len(cuts)))
        gain = gain * jnp.repeat(steps, shape[position] // shards_of).reshape([-1 if axis == position else 1 for axis in range(len(shape))])
    return gain


def centred(key, shape, scale, reach, pieces=(), kind=jnp.bfloat16):
    array = jax.random.normal(key, shape, jnp.float32) * scale
    if len(pieces) > 0:
        array = shard_levels(key, shape, pieces, -0.22, 0.18) * array
    return jnp.clip(array, min=-reach, max=reach).astype(kind)


def setup_inputs(seed: int = 0, part: int = 0) -> dict:
    seeds = jax.random.split(jax.random.key(seed), 13)
    part_splits = jax.random.split(jax.random.fold_in(seeds[12], part), 13)
    return {
        "segment_flow": centred(part_splits[0], (HOURS, SEGS, PIPES), 1.0, 4.0, ((0, 2), (1, 2), (2, 4)), jnp.float32),
        "linepack": jnp.clip(0.2 + 2.2 * jax.random.uniform(part_splits[1], (HOURS, SEGS, PIPES), jnp.float32) ** shard_levels(part_splits[1], (HOURS, SEGS, PIPES), ((0, 2), (1, 2), (2, 4)), -0.2, 0.2), 0.2, 2.4),
        "mass_dual": centred(part_splits[2], (HOURS, SEGS, PIPES), 0.5, 3.0, ((0, 2), (1, 2), (2, 4)), jnp.float32),
        "momentum_dual": centred(part_splits[3], (HOURS, SEGS, PIPES), 0.5, 3.0, ((0, 2), (1, 2), (2, 4)), jnp.float32),
        "contract_dual": centred(part_splits[4], (HOURS, SEG_PARTS, SEG_BLOCK, NC), 0.5, 3.0, ((0, 2), (1, 2), (2, 4)), jnp.float32),
        "flow_cost": draw_flow_cost(jax.random.fold_in(jax.random.fold_in(seeds[12], part), 71), part),
        "injection": centred(part_splits[6], (HOURS, SEGS, PIPES), 0.5, 3.0, ((0, 2), (1, 2), (2, 4)), jnp.float32),
        "contract_target": jnp.clip(0.4 + 1.6 * jax.random.uniform(part_splits[7], (HOURS, SEG_PARTS, SEG_BLOCK, NC), jnp.float32) ** shard_levels(part_splits[7], (HOURS, SEG_PARTS, SEG_BLOCK, NC), ((0, 2), (1, 2), (2, 4)), -0.2, 0.2), 0.4, 2.0),
        "friction_table": jnp.clip(jnp.exp(jax.random.uniform(seeds[8], (NCLS,), jnp.float32, math.log(0.3), math.log(3.0))), 0.3, 3.0),
        "friction_class": place_ends(jax.random.randint(part_splits[9], (SEGS, PIPES), 0, NCLS), jax.random.fold_in(part_splits[9], 1), 0, NCLS - 1).astype(jnp.int32),
        "matching": draw_matching(jax.random.fold_in(jax.random.fold_in(seeds[12], part), 71), part),
        "contract_map": place_ends(jax.random.randint(part_splits[11], (HOURS, PIPES), 0, NC), jax.random.fold_in(part_splits[11], 1), 0, NC - 1).astype(jnp.int32),
    }


FLOW_CAP = 1.5
PACK_CAP = 2.5
STEP_SCALE = 0.25
NORM_EPS = 1e-06

def contract_sums(linepack, contract_map):
    hour_count, seg_count, pipe_count = linepack.shape
    offsets = contract_map + NC * jnp.arange(hour_count, dtype=jnp.int32)[:, None]
    flattened = jnp.transpose(linepack, (0, 2, 1)).reshape(hour_count * pipe_count, seg_count)
    summed = jax.ops.segment_sum(flattened, offsets.reshape(-1), num_segments=hour_count * NC)
    return jnp.transpose(summed.reshape(hour_count, NC, seg_count), (0, 2, 1))

def contract_spread(duals, contract_map, seg_count):
    pick_index = jnp.broadcast_to(contract_map[:, None, :], (contract_map.shape[0], seg_count, contract_map.shape[1]))
    return jnp.take_along_axis(duals, pick_index, axis=2)

def forward(flow_bar, pack_bar, friction, matching, contract_map, share_scale):
    far_rows = jnp.take(flow_bar[:, -1, :], matching, axis=1)
    upstream = jnp.concatenate([far_rows[:, None, :], flow_bar[:, :-1, :]], axis=1)
    earlier = jnp.concatenate([jnp.zeros_like(pack_bar[:1]), pack_bar[:-1]], axis=0)
    after_seg = jnp.concatenate([pack_bar[:, 1:, :], jnp.zeros_like(pack_bar[:, :1])], axis=1)
    mass_rows = pack_bar - earlier + flow_bar - upstream
    momentum = friction * flow_bar - (pack_bar - after_seg)
    totals = share_scale * contract_sums(pack_bar, contract_map)
    return (mass_rows, momentum, totals)

def backward(mass_now, momentum_now, contract_now, friction, matching, contract_map, share_scale):
    returned = jnp.zeros_like(mass_now[:, 0, :]).at[:, matching].add(mass_now[:, 0, :])
    next_seg = jnp.concatenate([mass_now[:, 1:, :], returned[:, None, :]], axis=1)
    grad_flow = mass_now - next_seg + friction * momentum_now
    later_hour = jnp.concatenate([mass_now[1:], jnp.zeros_like(mass_now[:1])], axis=0)
    before_seg = jnp.concatenate([jnp.zeros_like(momentum_now[:, :1]), momentum_now[:, :-1]], axis=1)
    spread = contract_spread(contract_now, contract_map, SEGS)
    grad_pack = mass_now - later_hour - momentum_now + before_seg + share_scale * spread
    return (grad_flow, grad_pack)

def reference(segment_flow, linepack, mass_dual, momentum_dual, contract_dual, flow_cost, injection, contract_target, friction_table, friction_class, matching, contract_map):
    friction = jnp.take(friction_table, friction_class, axis=0)[None]
    share_scale = NC / PIPES
    target_now = contract_target.reshape(HOURS, SEGS, NC)
    contract_now = contract_dual.reshape(HOURS, SEGS, NC)
    weight = jnp.float32(1.0)
    for iteration in range(ITERS):
        primal_step = STEP_SCALE / weight
        dual_step = STEP_SCALE * weight
        grad_flow, grad_pack = backward(mass_dual, momentum_dual, contract_now, friction, matching, contract_map, share_scale)
        flow_next = jnp.clip(segment_flow - primal_step * (flow_cost - grad_flow), -FLOW_CAP, FLOW_CAP)
        pack_next = jnp.clip(linepack + primal_step * grad_pack, 0.0, PACK_CAP)
        mass_rows, momentum, totals = forward(2.0 * flow_next - segment_flow, 2.0 * pack_next - linepack, friction, matching, contract_map, share_scale)
        mass_next = mass_dual + dual_step * (injection - mass_rows)
        momentum_next = momentum_dual - dual_step * momentum
        contract_next = contract_now + dual_step * (target_now - totals)
        primal_sq = jnp.sum((flow_next - segment_flow) ** 2) + jnp.sum((pack_next - linepack) ** 2)
        dual_sq = jnp.sum((mass_next - mass_dual) ** 2) + jnp.sum((momentum_next - momentum_dual) ** 2) + jnp.sum((contract_next - contract_now) ** 2)
        weight = jnp.sqrt(weight * jnp.sqrt((dual_sq + NORM_EPS) / (primal_sq + NORM_EPS)))
        segment_flow, linepack = (flow_next, pack_next)
        mass_dual, momentum_dual, contract_now = (mass_next, momentum_next, contract_next)
    return (segment_flow, linepack, mass_dual, momentum_dual, contract_now.reshape(HOURS, SEG_PARTS, SEG_BLOCK, NC), weight.reshape(1))
```

```python
import functools

import jax
import jax.numpy as jnp
from jax import lax
from jax.experimental import pallas as pl
from jax.experimental.pallas import tpu as pltpu
from jax.sharding import PartitionSpec as P

ITERS = 2
FLOW_CAP = 1.5
PACK_CAP = 2.5
STEP_SCALE = 0.25
NORM_EPS = 1e-06
LANES = 128
PIECES = 3


def pieces_of(values):
    parts = []
    rest = values
    for _ in range(PIECES):
        part = rest.astype(jnp.bfloat16)
        rest = rest - part.astype(jnp.float32)
        parts.append(part.astype(jnp.float32))
    return jnp.concatenate(parts, axis=0).astype(jnp.bfloat16)


def joined(stacked, rows):
    total = stacked[(PIECES - 1) * rows :]
    for piece in range(PIECES - 2, -1, -1):
        total = total + stacked[piece * rows : (piece + 1) * rows]
    return total


def folded(cells):
    rows, columns = cells.shape
    total = None
    for row in range(0, rows, 8):
        for column in range(0, columns, LANES):
            block = cells[row : row + 8, column : column + LANES]
            total = block if total is None else total + block
    return total


def kernel(
    sizes,
    table_ref,
    flow_in, pack_in, mass_in, mom_in, dual_in, cost_in, inj_in, target_in, class_in, match_in, map_in,
    flow_out, pack_out, mass_out, mom_out, dual_out, weight_out,
    flow, pack, mass, mom, dual, cost, inj, target, classes, match, cmap,
    fric, flow_bar, pack_bar, onehot_c, onehot_m,
    row_send, row_recv, hour_recv, sum_send, sum_recv, dual_recv, norm_send, norm_recv,
    in_sem, out_sem, row_ss, row_rs, hour_ss, hour_rs, sum_ss, sum_rs, dual_ss, dual_rs, norm_ss, norm_rs,
):
    pipes, hours, segs, H, S, W, C, R, T = sizes
    share = C / T
    peers = pipes * hours * segs
    me_p, me_h, me_s = lax.axis_index("pipe"), lax.axis_index("hour"), lax.axis_index("seg")
    me = (me_p * hours + me_h) * segs + me_s
    other_s = lax.rem(me_s + 1, segs)
    first_half, last_half = me_s == 0, me_s == segs - 1
    first_hour, last_hour = me_h == 0, me_h == hours - 1

    def load(index, source, place):
        copy = pltpu.make_async_copy(source, place, in_sem.at[index])
        copy.start()
        return copy

    get_mass = load(0, mass_in, mass.at[0])
    get_mom = load(1, mom_in, mom.at[0])
    get_dual = load(2, dual_in, dual.at[0])
    get_match = load(3, match_in, match)
    get_map = load(4, map_in, cmap)
    get_class = load(5, class_in, classes)
    get_flow = load(6, flow_in, flow.at[0])
    get_pack = load(7, pack_in, pack.at[0])
    get_cost = load(8, cost_in, cost)
    get_inj = load(9, inj_in, inj)
    get_target = load(10, target_in, target)

    def peer(step):
        dp, rest = step // (hours * segs), step % (hours * segs)
        return {
            "pipe": lax.rem(me_p + dp, pipes),
            "hour": lax.rem(me_h + rest // segs, hours),
            "seg": lax.rem(me_s + rest % segs, segs),
        }

    def each_peer(act):
        if peers <= 32:
            for step in range(1, peers):
                act(step)
        else:
            def body(step, carry):
                act(step)
                return carry
            lax.fori_loop(1, peers, body, 0)

    barrier = pltpu.get_barrier_semaphore()

    def greet(step):
        pl.semaphore_signal(barrier, inc=1, device_id=peer(step), device_id_type=pl.DeviceIdType.MESH)

    each_peer(greet)

    sent = []

    def remote(source, place, send_sem, recv_sem, where):
        copy = pltpu.make_async_remote_copy(
            src_ref=source, dst_ref=place, send_sem=send_sem, recv_sem=recv_sem,
            device_id=where, device_id_type=pl.DeviceIdType.MESH,
        )
        copy.start()
        sent.append(copy)
        return copy

    def send_rows(turn):
        return [
            remote(
                row_send.at[turn], row_recv.at[turn, me_p], row_ss.at[turn, step], row_rs.at[turn, step],
                {"pipe": lax.rem(me_p + step, pipes), "seg": other_s},
            )
            for step in range(pipes)
        ]

    def send_duals(it):
        dual_recv[it, me_p] = dual[it]
        return [
            remote(
                dual.at[it], dual_recv.at[it, me_p], dual_ss.at[it, step], dual_rs.at[it, step],
                {"pipe": lax.rem(me_p + step, pipes)},
            )
            for step in range(1, pipes)
        ]

    def send_sums(it):
        return [
            remote(
                sum_send.at[it, lax.rem(me_p + step, pipes)], sum_recv.at[it, me_p],
                sum_ss.at[it, step], sum_rs.at[it, step],
                {"pipe": lax.rem(me_p + step, pipes)},
            )
            for step in range(1, pipes)
        ]

    def norm_copy(it, step):
        return pltpu.make_async_remote_copy(
            src_ref=norm_send.at[it], dst_ref=norm_recv.at[it, me],
            send_sem=norm_ss.at[it, step], recv_sem=norm_rs.at[it, step],
            device_id=peer(step), device_id_type=pl.DeviceIdType.MESH,
        )

    def fill_dual_rows(it, turn):
        for h in range(H):
            row_send[turn, h : h + 1, :] = mass[it, h, 0:1, :]
            row_send[turn, H + h : H + h + 1, :] = mom[it, h, S - 1 : S, :]

    def send_dual_halo(it, turn):
        rows = send_rows(turn)
        layer = remote(
            mass.at[it, 0], hour_recv.at[turn], hour_ss.at[turn], hour_rs.at[turn],
            {"hour": lax.rem(me_h + hours - 1, hours)},
        )
        return rows + [layer]

    get_mass.wait()
    get_mom.wait()
    fill_dual_rows(0, 0)
    get_dual.wait()
    pl.semaphore_wait(barrier, peers - 1)
    waiting_duals = send_duals(0)
    waiting_halo = send_dual_halo(0, 0)

    get_map.wait()
    start = pl.multiple_of(me_p * W, LANES)
    own_map = cmap[:, pl.ds(start, W)]
    class_rows = lax.broadcasted_iota(jnp.int32, (C, W), 0)
    for h in range(H):
        onehot_c[h] = jnp.where(own_map[h : h + 1, :] == class_rows, 1.0, 0.0).astype(jnp.bfloat16)
    get_match.wait()

    @pl.when(first_half)
    def _():
        wanted = match[:, pl.ds(start, W)]
        rows = lax.broadcasted_iota(jnp.int32, (LANES, W), 0)
        for block in range(0, T, LANES):
            hit = wanted == rows + block
            onehot_m[block : block + LANES, :] = jnp.where(hit, 1.0, 0.0).astype(jnp.bfloat16)

    @pl.when(jnp.logical_not(first_half))
    def _():
        columns = lax.broadcasted_iota(jnp.int32, (LANES, W), 1).astype(jnp.float32)
        columns = columns + start.astype(jnp.float32)
        for block in range(0, T, LANES):
            line = match[:, block : block + LANES].astype(jnp.float32)
            upright = jnp.transpose(jnp.broadcast_to(line, (LANES, LANES)))
            hit = jnp.concatenate([upright] * (W // LANES), axis=1) == columns
            onehot_m[block : block + LANES, :] = jnp.where(hit, 1.0, 0.0).astype(jnp.bfloat16)

    get_class.wait()
    kinds = classes[...]
    level = jnp.zeros((S, W), jnp.float32)
    for kind in range(table_ref.shape[0]):
        level = jnp.where(kinds == kind, table_ref[kind], level)
    fric[...] = level

    def matched_rows(turn):
        line = jnp.concatenate([row_recv[turn, block] for block in range(pipes)], axis=1)
        found = jnp.dot(pieces_of(line), onehot_m[...], preferred_element_type=jnp.float32)
        return joined(found, 2 * H)

    seg_at = lax.broadcasted_iota(jnp.int32, (S, W), 0)
    top, bottom = seg_at == 0, seg_at == S - 1
    get_flow.wait()
    get_pack.wait()
    get_cost.wait()

    outgoing = []

    def put(index, source, place):
        copy = pltpu.make_async_copy(source, place, out_sem.at[index])
        copy.start()
        outgoing.append(copy)

    weight = None
    for it in range(ITERS):
        turn = 2 * it
        for copy in waiting_halo:
            copy.wait_recv()
        found = matched_rows(turn)
        near = row_recv[turn, me_p]
        next_row = jnp.where(first_half, near, found)
        before_row = jnp.where(first_half, 0.0, near)
        for copy in waiting_duals:
            copy.wait_recv()
        spreads = []
        for h in range(H):
            held = jnp.concatenate([dual_recv[it, block, h] for block in range(pipes)], axis=0)
            spreads.append(
                joined(jnp.dot(pieces_of(held), onehot_c[h], preferred_element_type=jnp.float32), S)
            )
        if it == 0:
            primal_step, dual_step = STEP_SCALE, STEP_SCALE
        else:
            weight = finish_norms(it - 1, weight)
            primal_step, dual_step = STEP_SCALE / weight, STEP_SCALE * weight
        primal_sq = jnp.zeros((S, W), jnp.float32)
        for h in range(H):
            m, r = mass[it, h], mom[it, h]
            later = mass[it, h + 1] if h < H - 1 else jnp.where(last_hour, 0.0, hour_recv[turn])
            next_seg = jnp.where(bottom, next_row[h : h + 1], pltpu.roll(m, S - 1, 0))
            before = jnp.where(top, before_row[H + h : H + h + 1], pltpu.roll(r, 1, 0))
            grad_flow = m - next_seg + fric[...] * r
            grad_pack = m - later - r + before + share * spreads[h]
            f, q = flow[it, h], pack[it, h]
            flow_next = jnp.clip(f - primal_step * (cost[h] - grad_flow), -FLOW_CAP, FLOW_CAP)
            pack_next = jnp.clip(q + primal_step * grad_pack, 0.0, PACK_CAP)
            flow[it + 1, h] = flow_next
            pack[it + 1, h] = pack_next
            fb, pb = 2.0 * flow_next - f, 2.0 * pack_next - q
            flow_bar[it, h] = fb
            pack_bar[it, h] = pb
            row_send[turn + 1, h : h + 1, :] = fb[S - 1 : S]
            row_send[turn + 1, H + h : H + h + 1, :] = pb[0:1]
            primal_sq = primal_sq + (flow_next - f) ** 2 + (pack_next - q) ** 2
            partial = joined(
                lax.dot_general(
                    pieces_of(pb), onehot_c[h], (((1,), (1,)), ((), ())),
                    preferred_element_type=jnp.float32,
                ),
                S,
            )
            for block in range(pipes):
                sum_send[it, block, h] = partial[block * R : (block + 1) * R]
        waiting_sums = send_sums(it)
        waiting_halo = send_rows(turn + 1)
        waiting_halo.append(
            remote(
                pack_bar.at[it, H - 1], hour_recv.at[turn + 1], hour_ss.at[turn + 1], hour_rs.at[turn + 1],
                {"hour": lax.rem(me_h + 1, hours)},
            )
        )
        if it == ITERS - 1:
            put(0, flow.at[ITERS], flow_out)
            put(1, pack.at[ITERS], pack_out)
        primal_block = folded(primal_sq)
        sum_recv[it, me_p] = sum_send[it, me_p]
        if it == 0:
            get_inj.wait()
            get_target.wait()
        for copy in waiting_halo:
            copy.wait_recv()
        found = matched_rows(turn + 1)
        near = row_recv[turn + 1, me_p]
        first_row = jnp.where(first_half, found, near)
        after_row = jnp.where(last_half, 0.0, near)
        dual_sq = jnp.zeros((S, W), jnp.float32)
        for h in range(H):
            fb, pb = flow_bar[it, h], pack_bar[it, h]
            m, r = mass[it, h], mom[it, h]
            earlier = pack_bar[it, h - 1] if h > 0 else jnp.where(first_hour, 0.0, hour_recv[turn + 1])
            upstream = jnp.where(top, first_row[h : h + 1], pltpu.roll(fb, 1, 0))
            after = jnp.where(bottom, after_row[H + h : H + h + 1], pltpu.roll(pb, S - 1, 0))
            mass_next = m + dual_step * (inj[h] - (pb - earlier + fb - upstream))
            mom_next = r - dual_step * (fric[...] * fb - (pb - after))
            mass[it + 1, h] = mass_next
            mom[it + 1, h] = mom_next
            dual_sq = dual_sq + (mass_next - m) ** 2 + (mom_next - r) ** 2
        if it < ITERS - 1:
            fill_dual_rows(it + 1, turn + 2)
            waiting_halo = send_dual_halo(it + 1, turn + 2)
        else:
            put(2, mass.at[ITERS], mass_out)
            put(3, mom.at[ITERS], mom_out)
        dual_block = folded(dual_sq)
        for copy in waiting_sums:
            copy.wait_recv()
        totals = sum_recv[it, 0]
        for block in range(1, pipes):
            totals = totals + sum_recv[it, block]
        held = dual[it]
        dual_next = held + dual_step * (target[...] - share * totals)
        dual[it + 1] = dual_next
        if it < ITERS - 1:
            waiting_duals = send_duals(it + 1)
        else:
            put(4, dual.at[ITERS], dual_out)
        change = (dual_next - held) ** 2
        lines = jnp.sum(change, axis=0)
        if R % 8 == 0:
            dual_block = dual_block + folded(lines)
        else:
            spot = lax.broadcasted_iota(jnp.int32, (8, C), 0) == 0
            dual_block = dual_block + jnp.where(spot, jnp.sum(lines, axis=0, keepdims=True), 0.0)
        upper = lax.broadcasted_iota(jnp.int32, (8, LANES), 0) < 4
        both = jnp.where(
            upper, primal_block + pltpu.roll(primal_block, 4, 0), dual_block + pltpu.roll(dual_block, 4, 0)
        )
        norm_send[it] = both
        norm_recv[it, me] = both
        each_peer(lambda step: norm_copy(it, step).start())

        def finish_norms(it, weight):
            each_peer(lambda step: norm_copy(it, step).wait_recv())
            total = jnp.sum(norm_recv[it], axis=0)
            primal = jnp.sum(jnp.where(upper, total, 0.0), axis=(0, 1), keepdims=True)
            dual_all = jnp.sum(jnp.where(upper, 0.0, total), axis=(0, 1), keepdims=True)
            ratio = jnp.sqrt((dual_all + NORM_EPS) / (primal + NORM_EPS))
            return jnp.sqrt(ratio if weight is None else weight * ratio)

    weight = finish_norms(ITERS - 1, weight)
    weight_out[0] = jnp.sum(weight)
    for copy in sent:
        copy.wait_send()
    for it in range(ITERS):
        each_peer(lambda step: norm_copy(it, step).wait_send())
    for copy in outgoing:
        copy.wait()


def on_device(
    segment_flow, linepack, mass_dual, momentum_dual, contract_dual, flow_cost, injection, contract_target,
    friction_table, friction_class, matching, contract_map,
):
    H, S, W = segment_flow.shape
    C = contract_dual.shape[3]
    R = contract_dual.shape[2]
    pipes, hours, segs = lax.axis_size("pipe"), lax.axis_size("hour"), lax.axis_size("seg")
    peers = pipes * hours * segs
    T = W * pipes
    f32, i32 = jnp.float32, jnp.int32
    anywhere = pl.BlockSpec(memory_space=pl.ANY)
    smem = pl.BlockSpec(memory_space=pltpu.SMEM)
    cells = jax.ShapeDtypeStruct((H, S, W), f32)
    turns = 2 * ITERS
    dma = pltpu.SemaphoreType.DMA
    outs = pl.pallas_call(
        functools.partial(kernel, (pipes, hours, segs, H, S, W, C, R, T)),
        out_shape=(cells,) * 4
        + (jax.ShapeDtypeStruct((H, R, C), f32), jax.ShapeDtypeStruct((1,), f32)),
        in_specs=[smem] + [anywhere] * 11,
        out_specs=(anywhere,) * 5 + (smem,),
        scratch_shapes=[
            pltpu.VMEM((ITERS + 1, H, S, W), f32),
            pltpu.VMEM((ITERS + 1, H, S, W), f32),
            pltpu.VMEM((ITERS + 1, H, S, W), f32),
            pltpu.VMEM((ITERS + 1, H, S, W), f32),
            pltpu.VMEM((ITERS + 1, H, R, C), f32),
            pltpu.VMEM((H, S, W), f32),
            pltpu.VMEM((H, S, W), f32),
            pltpu.VMEM((H, R, C), f32),
            pltpu.VMEM((S, W), i32),
            pltpu.VMEM((1, T), i32),
            pltpu.VMEM((H, T), i32),
            pltpu.VMEM((S, W), f32),
            pltpu.VMEM((ITERS, H, S, W), f32),
            pltpu.VMEM((ITERS, H, S, W), f32),
            pltpu.VMEM((H, C, W), jnp.bfloat16),
            pltpu.VMEM((T, W), jnp.bfloat16),
            pltpu.VMEM((turns, 2 * H, W), f32),
            pltpu.VMEM((turns, pipes, 2 * H, W), f32),
            pltpu.VMEM((turns, S, W), f32),
            pltpu.VMEM((ITERS, pipes, H, R, C), f32),
            pltpu.VMEM((ITERS, pipes, H, R, C), f32),
            pltpu.VMEM((ITERS, pipes, H, R, C), f32),
            pltpu.VMEM((ITERS, 8, LANES), f32),
            pltpu.VMEM((ITERS, peers, 8, LANES), f32),
            dma((11,)),
            dma((5,)),
            dma((turns, pipes)),
            dma((turns, pipes)),
            dma((turns,)),
            dma((turns,)),
            dma((ITERS, pipes)),
            dma((ITERS, pipes)),
            dma((ITERS, pipes)),
            dma((ITERS, pipes)),
            dma((ITERS, peers)),
            dma((ITERS, peers)),
        ],
        compiler_params=pltpu.CompilerParams(
            collective_id=0, has_side_effects=True, vmem_limit_bytes=48 * 1024 * 1024
        ),
        cost_estimate=pl.CostEstimate(flops=10**8, bytes_accessed=2 * 10**6, transcendentals=0),
    )(
        friction_table, segment_flow, linepack, mass_dual, momentum_dual, contract_dual.reshape(H, R, C),
        flow_cost, injection, contract_target.reshape(H, R, C), friction_class, matching.reshape(1, T),
        contract_map,
    )
    return outs[:4] + (outs[4].reshape(contract_dual.shape), outs[5])


def solution(mesh):
    cells = P(("groups", "hour"), "seg", "pipe")
    contracts = P(("groups", "hour"), "seg", "pipe", None)
    return jax.shard_map(
        on_device,
        mesh=mesh,
        in_specs=(
            cells, cells, cells, cells, contracts, cells, cells, contracts,
            P(), P("seg", ("groups", "pipe")), P("groups"), P(("groups", "hour"), None),
        ),
        out_specs=(cells, cells, cells, cells, contracts, P("groups")),
        check_vma=False,
    )
```

```python
import functools

import jax
import jax.numpy as jnp
from jax import lax
from jax.experimental import pallas as pl
from jax.experimental.pallas import tpu as pltpu
from jax.sharding import PartitionSpec as P

ITERS = 2
FLOW_CAP = 1.5
PACK_CAP = 2.5
STEP_SCALE = 0.25
NORM_EPS = 1e-06
LANES = 128
PIECES = 3


def pieces_of(values):
    parts = []
    rest = values
    for _ in range(PIECES):
        part = rest.astype(jnp.bfloat16)
        rest = rest - part.astype(jnp.float32)
        parts.append(part.astype(jnp.float32))
    return jnp.concatenate(parts, axis=0).astype(jnp.bfloat16)


def joined(stacked, rows):
    total = stacked[(PIECES - 1) * rows :]
    for piece in range(PIECES - 2, -1, -1):
        total = total + stacked[piece * rows : (piece + 1) * rows]
    return total


def folded(cells):
    rows, columns = cells.shape
    total = None
    for row in range(0, rows, 8):
        for column in range(0, columns, LANES):
            block = cells[row : row + 8, column : column + LANES]
            total = block if total is None else total + block
    return total


def kernel(
    sizes,
    table_ref,
    flow_in, pack_in, mass_in, mom_in, dual_in, cost_in, inj_in, target_in, class_in, match_in, map_in,
    flow_out, pack_out, mass_out, mom_out, dual_out, weight_out,
    flow, pack, mass, mom, dual, cost, inj, target, classes, match, cmap,
    fric, flow_bar, pack_bar, onehot_c, onehot_m,
    row_send, row_recv, hour_recv, sum_send, sum_recv, dual_recv, norm_send, norm_recv,
    in_sem, out_sem, row_ss, row_rs, hour_ss, hour_rs, sum_ss, sum_rs, dual_ss, dual_rs, norm_ss, norm_rs,
):
    pipes, hours, segs, H, S, W, C, R, T = sizes
    share = C / T
    peers = pipes * hours * segs
    me_p, me_h, me_s = lax.axis_index("pipe"), lax.axis_index("hour"), lax.axis_index("seg")
    me = (me_p * hours + me_h) * segs + me_s
    other_s = lax.rem(me_s + 1, segs)
    first_half, last_half = me_s == 0, me_s == segs - 1
    first_hour, last_hour = me_h == 0, me_h == hours - 1

    def load(index, source, place):
        copy = pltpu.make_async_copy(source, place, in_sem.at[index])
        copy.start()
        return copy

    get_mass = load(0, mass_in, mass.at[0])
    get_mom = load(1, mom_in, mom.at[0])
    get_dual = load(2, dual_in, dual.at[0])
    get_match = load(3, match_in, match)
    get_map = load(4, map_in, cmap)
    get_class = load(5, class_in, classes)
    get_flow = load(6, flow_in, flow.at[0])
    get_pack = load(7, pack_in, pack.at[0])
    get_cost = load(8, cost_in, cost)
    get_inj = load(9, inj_in, inj)
    get_target = load(10, target_in, target)

    def peer(step):
        dp, rest = step // (hours * segs), step % (hours * segs)
        return {
            "pipe": lax.rem(me_p + dp, pipes),
            "hour": lax.rem(me_h + rest // segs, hours),
            "seg": lax.rem(me_s + rest % segs, segs),
        }

    def each_peer(act):
        if peers <= 32:
            for step in range(1, peers):
                act(step)
        else:
            def body(step, carry):
                act(step)
                return carry
            lax.fori_loop(1, peers, body, 0)

    barrier = pltpu.get_barrier_semaphore()

    def greet(step):
        pl.semaphore_signal(barrier, inc=1, device_id=peer(step), device_id_type=pl.DeviceIdType.MESH)

    each_peer(greet)

    sent = []

    def remote(source, place, send_sem, recv_sem, where):
        copy = pltpu.make_async_remote_copy(
            src_ref=source, dst_ref=place, send_sem=send_sem, recv_sem=recv_sem,
            device_id=where, device_id_type=pl.DeviceIdType.MESH,
        )
        copy.start()
        sent.append(copy)
        return copy

    def send_rows(turn):
        return [
            remote(
                row_send.at[turn], row_recv.at[turn, me_p], row_ss.at[turn, step], row_rs.at[turn, step],
                {"pipe": lax.rem(me_p + step, pipes), "seg": other_s},
            )
            for step in range(pipes)
        ]

    def send_duals(it):
        dual_recv[it, me_p] = dual[it]
        return [
            remote(
                dual.at[it], dual_recv.at[it, me_p], dual_ss.at[it, step], dual_rs.at[it, step],
                {"pipe": lax.rem(me_p + step, pipes)},
            )
            for step in range(1, pipes)
        ]

    def send_sums(it):
        return [
            remote(
                sum_send.at[it, lax.rem(me_p + step, pipes)], sum_recv.at[it, me_p],
                sum_ss.at[it, step], sum_rs.at[it, step],
                {"pipe": lax.rem(me_p + step, pipes)},
            )
            for step in range(1, pipes)
        ]

    def norm_copy(it, step):
        return pltpu.make_async_remote_copy(
            src_ref=norm_send.at[it], dst_ref=norm_recv.at[it, me],
            send_sem=norm_ss.at[it, step], recv_sem=norm_rs.at[it, step],
            device_id=peer(step), device_id_type=pl.DeviceIdType.MESH,
        )

    def fill_dual_rows(it, turn):
        for h in range(H):
            row_send[turn, h : h + 1, :] = mass[it, h, 0:1, :]
            row_send[turn, H + h : H + h + 1, :] = mom[it, h, S - 1 : S, :]

    def send_dual_halo(it, turn):
        rows = send_rows(turn)
        layer = remote(
            mass.at[it, 0], hour_recv.at[turn], hour_ss.at[turn], hour_rs.at[turn],
            {"hour": lax.rem(me_h + hours - 1, hours)},
        )
        return rows + [layer]

    get_mass.wait()
    get_mom.wait()
    fill_dual_rows(0, 0)
    get_dual.wait()
    pl.semaphore_wait(barrier, peers - 1)
    waiting_duals = send_duals(0)
    waiting_halo = send_dual_halo(0, 0)

    get_map.wait()
    start = pl.multiple_of(me_p * W, LANES)
    own_map = cmap[:, pl.ds(start, W)]
    class_rows = lax.broadcasted_iota(jnp.int32, (C, W), 0)
    for h in range(H):
        onehot_c[h] = jnp.where(own_map[h : h + 1, :] == class_rows, 1.0, 0.0).astype(jnp.bfloat16)
    get_match.wait()

    @pl.when(first_half)
    def _():
        wanted = match[:, pl.ds(start, W)]
        rows = lax.broadcasted_iota(jnp.int32, (LANES, W), 0)
        for block in range(0, T, LANES):
            hit = wanted == rows + block
            onehot_m[block : block + LANES, :] = jnp.where(hit, 1.0, 0.0).astype(jnp.bfloat16)

    @pl.when(jnp.logical_not(first_half))
    def _():
        columns = lax.broadcasted_iota(jnp.int32, (LANES, W), 1).astype(jnp.float32)
        columns = columns + start.astype(jnp.float32)
        for block in range(0, T, LANES):
            line = match[:, block : block + LANES].astype(jnp.float32)
            upright = jnp.transpose(jnp.broadcast_to(line, (LANES, LANES)))
            hit = jnp.concatenate([upright] * (W // LANES), axis=1) == columns
            onehot_m[block : block + LANES, :] = jnp.where(hit, 1.0, 0.0).astype(jnp.bfloat16)

    get_class.wait()
    kinds = classes[...]
    level = jnp.zeros((S, W), jnp.float32)
    for kind in range(table_ref.shape[0]):
        level = jnp.where(kinds == kind, table_ref[kind], level)
    fric[...] = level

    def matched_rows(turn):
        line = jnp.concatenate([row_recv[turn, block] for block in range(pipes)], axis=1)
        found = jnp.dot(pieces_of(line), onehot_m[...], preferred_element_type=jnp.float32)
        return joined(found, 2 * H)

    seg_at = lax.broadcasted_iota(jnp.int32, (S, W), 0)
    top, bottom = seg_at == 0, seg_at == S - 1
    get_flow.wait()
    get_pack.wait()
    get_cost.wait()

    outgoing = []

    def put(index, source, place):
        copy = pltpu.make_async_copy(source, place, out_sem.at[index])
        copy.start()
        outgoing.append(copy)

    weight = None
    for it in range(ITERS):
        turn = 2 * it
        for copy in waiting_halo:
            copy.wait_recv()
        found = matched_rows(turn)
        near = row_recv[turn, me_p]
        next_row = jnp.where(first_half, near, found)
        before_row = jnp.where(first_half, 0.0, near)
        for copy in waiting_duals:
            copy.wait_recv()
        spreads = []
        for h in range(H):
            held = jnp.concatenate([dual_recv[it, block, h] for block in range(pipes)], axis=0)
            spreads.append(
                joined(jnp.dot(pieces_of(held), onehot_c[h], preferred_element_type=jnp.float32), S)
            )
        if it == 0:
            primal_step, dual_step = STEP_SCALE, STEP_SCALE
        else:
            weight = finish_norms(it - 1, weight)
            primal_step, dual_step = STEP_SCALE / weight, STEP_SCALE * weight
        primal_sq = jnp.zeros((S, W), jnp.float32)
        for h in range(H):
            m, r = mass[it, h], mom[it, h]
            later = mass[it, h + 1] if h < H - 1 else jnp.where(last_hour, 0.0, hour_recv[turn])
            next_seg = jnp.where(bottom, next_row[h : h + 1], pltpu.roll(m, S - 1, 0))
            before = jnp.where(top, before_row[H + h : H + h + 1], pltpu.roll(r, 1, 0))
            grad_flow = m - next_seg + fric[...] * r
            grad_pack = m - later - r + before + share * spreads[h]
            f, q = flow[it, h], pack[it, h]
            flow_next = jnp.clip(f - primal_step * (cost[h] - grad_flow), -FLOW_CAP, FLOW_CAP)
            pack_next = jnp.clip(q + primal_step * grad_pack, 0.0, PACK_CAP)
            flow[it + 1, h] = flow_next
            pack[it + 1, h] = pack_next
            fb, pb = 2.0 * flow_next - f, 2.0 * pack_next - q
            flow_bar[it, h] = fb
            pack_bar[it, h] = pb
            row_send[turn + 1, h : h + 1, :] = fb[S - 1 : S]
            row_send[turn + 1, H + h : H + h + 1, :] = pb[0:1]
            primal_sq = primal_sq + (flow_next - f) ** 2 + (pack_next - q) ** 2
            partial = joined(
                lax.dot_general(
                    pieces_of(pb), onehot_c[h], (((1,), (1,)), ((), ())),
                    preferred_element_type=jnp.float32,
                ),
                S,
            )
            for block in range(pipes):
                sum_send[it, block, h] = partial[block * R : (block + 1) * R]
        waiting_sums = send_sums(it)
        waiting_halo = send_rows(turn + 1)
        waiting_halo.append(
            remote(
                pack_bar.at[it, H - 1], hour_recv.at[turn + 1], hour_ss.at[turn + 1], hour_rs.at[turn + 1],
                {"hour": lax.rem(me_h + 1, hours)},
            )
        )
        if it == ITERS - 1:
            put(0, flow.at[ITERS], flow_out)
            put(1, pack.at[ITERS], pack_out)
        primal_block = folded(primal_sq)
        sum_recv[it, me_p] = sum_send[it, me_p]
        if it == 0:
            get_inj.wait()
            get_target.wait()
        for copy in waiting_halo:
            copy.wait_recv()
        found = matched_rows(turn + 1)
        near = row_recv[turn + 1, me_p]
        first_row = jnp.where(first_half, found, near)
        after_row = jnp.where(last_half, 0.0, near)
        dual_sq = jnp.zeros((S, W), jnp.float32)
        for h in range(H):
            fb, pb = flow_bar[it, h], pack_bar[it, h]
            m, r = mass[it, h], mom[it, h]
            earlier = pack_bar[it, h - 1] if h > 0 else jnp.where(first_hour, 0.0, hour_recv[turn + 1])
            upstream = jnp.where(top, first_row[h : h + 1], pltpu.roll(fb, 1, 0))
            after = jnp.where(bottom, after_row[H + h : H + h + 1], pltpu.roll(pb, S - 1, 0))
            mass_next = m + dual_step * (inj[h] - (pb - earlier + fb - upstream))
            mom_next = r - dual_step * (fric[...] * fb - (pb - after))
            mass[it + 1, h] = mass_next
            mom[it + 1, h] = mom_next
            dual_sq = dual_sq + (mass_next - m) ** 2 + (mom_next - r) ** 2
        if it < ITERS - 1:
            fill_dual_rows(it + 1, turn + 2)
            waiting_halo = send_dual_halo(it + 1, turn + 2)
        else:
            put(2, mass.at[ITERS], mass_out)
            put(3, mom.at[ITERS], mom_out)
        dual_block = folded(dual_sq)
        for copy in waiting_sums:
            copy.wait_recv()
        totals = sum_recv[it, 0]
        for block in range(1, pipes):
            totals = totals + sum_recv[it, block]
        held = dual[it]
        dual_next = held + dual_step * (target[...] - share * totals)
        dual[it + 1] = dual_next
        if it < ITERS - 1:
            waiting_duals = send_duals(it + 1)
        else:
            put(4, dual.at[ITERS], dual_out)
        change = (dual_next - held) ** 2
        lines = jnp.sum(change, axis=0)
        if R % 8 == 0:
            dual_block = dual_block + folded(lines)
        else:
            spot = lax.broadcasted_iota(jnp.int32, (8, C), 0) == 0
            dual_block = dual_block + jnp.where(spot, jnp.sum(lines, axis=0, keepdims=True), 0.0)
        upper = lax.broadcasted_iota(jnp.int32, (8, LANES), 0) < 4
        both = jnp.where(
            upper, primal_block + pltpu.roll(primal_block, 4, 0), dual_block + pltpu.roll(dual_block, 4, 0)
        )
        norm_send[it] = both
        norm_recv[it, me] = both
        each_peer(lambda step: norm_copy(it, step).start())

        def finish_norms(it, weight):
            each_peer(lambda step: norm_copy(it, step).wait_recv())
            total = jnp.sum(norm_recv[it], axis=0)
            primal = jnp.sum(jnp.where(upper, total, 0.0), axis=(0, 1), keepdims=True)
            dual_all = jnp.sum(jnp.where(upper, 0.0, total), axis=(0, 1), keepdims=True)
            ratio = jnp.sqrt((dual_all + NORM_EPS) / (primal + NORM_EPS))
            return jnp.sqrt(ratio if weight is None else weight * ratio)

    weight = finish_norms(ITERS - 1, weight)
    weight_out[0] = jnp.sum(weight)
    for copy in sent:
        copy.wait_send()
    for it in range(ITERS):
        each_peer(lambda step: norm_copy(it, step).wait_send())
    for copy in outgoing:
        copy.wait()


def store_kernel(*refs):
    count = (len(refs) - 1) // 2
    sem = refs[-1]
    copies = [pltpu.make_async_copy(refs[i], refs[count + i], sem.at[i]) for i in range(count)]
    for copy in copies:
        copy.start()
    for copy in copies:
        copy.wait()


def on_device(
    segment_flow, linepack, mass_dual, momentum_dual, contract_dual, flow_cost, injection, contract_target,
    friction_table, friction_class, matching, contract_map,
):
    H, S, W = segment_flow.shape
    C = contract_dual.shape[3]
    R = contract_dual.shape[2]
    pipes, hours, segs = lax.axis_size("pipe"), lax.axis_size("hour"), lax.axis_size("seg")
    peers = pipes * hours * segs
    T = W * pipes
    f32, i32 = jnp.float32, jnp.int32
    anywhere = pl.BlockSpec(memory_space=pl.ANY)
    hbm = pl.BlockSpec(memory_space=pltpu.HBM)
    smem = pl.BlockSpec(memory_space=pltpu.SMEM)
    cells = jax.ShapeDtypeStruct((H, S, W), f32)
    turns = 2 * ITERS
    dma = pltpu.SemaphoreType.DMA
    outs = pl.pallas_call(
        functools.partial(kernel, (pipes, hours, segs, H, S, W, C, R, T)),
        out_shape=(cells,) * 4
        + (jax.ShapeDtypeStruct((H, R, C), f32), jax.ShapeDtypeStruct((1,), f32)),
        in_specs=[smem] + [hbm] * 11,
        out_specs=(anywhere,) * 5 + (smem,),
        scratch_shapes=[
            pltpu.VMEM((ITERS + 1, H, S, W), f32),
            pltpu.VMEM((ITERS + 1, H, S, W), f32),
            pltpu.VMEM((ITERS + 1, H, S, W), f32),
            pltpu.VMEM((ITERS + 1, H, S, W), f32),
            pltpu.VMEM((ITERS + 1, H, R, C), f32),
            pltpu.VMEM((H, S, W), f32),
            pltpu.VMEM((H, S, W), f32),
            pltpu.VMEM((H, R, C), f32),
            pltpu.VMEM((S, W), i32),
            pltpu.VMEM((1, T), i32),
            pltpu.VMEM((H, T), i32),
            pltpu.VMEM((S, W), f32),
            pltpu.VMEM((ITERS, H, S, W), f32),
            pltpu.VMEM((ITERS, H, S, W), f32),
            pltpu.VMEM((H, C, W), jnp.bfloat16),
            pltpu.VMEM((T, W), jnp.bfloat16),
            pltpu.VMEM((turns, 2 * H, W), f32),
            pltpu.VMEM((turns, pipes, 2 * H, W), f32),
            pltpu.VMEM((turns, S, W), f32),
            pltpu.VMEM((ITERS, pipes, H, R, C), f32),
            pltpu.VMEM((ITERS, pipes, H, R, C), f32),
            pltpu.VMEM((ITERS, pipes, H, R, C), f32),
            pltpu.VMEM((ITERS, 8, LANES), f32),
            pltpu.VMEM((ITERS, peers, 8, LANES), f32),
            dma((11,)),
            dma((5,)),
            dma((turns, pipes)),
            dma((turns, pipes)),
            dma((turns,)),
            dma((turns,)),
            dma((ITERS, pipes)),
            dma((ITERS, pipes)),
            dma((ITERS, pipes)),
            dma((ITERS, pipes)),
            dma((ITERS, peers)),
            dma((ITERS, peers)),
        ],
        compiler_params=pltpu.CompilerParams(
            collective_id=0, has_side_effects=True, vmem_limit_bytes=63 * 1024 * 1024
        ),
        cost_estimate=pl.CostEstimate(flops=10**8, bytes_accessed=2 * 10**6, transcendentals=0),
    )(
        friction_table, segment_flow, linepack, mass_dual, momentum_dual, contract_dual.reshape(H, R, C),
        flow_cost, injection, contract_target.reshape(H, R, C), friction_class, matching.reshape(1, T),
        contract_map,
    )
    stored = pl.pallas_call(
        store_kernel,
        out_shape=(cells,) * 4 + (jax.ShapeDtypeStruct((H, R, C), f32),),
        in_specs=[anywhere] * 5,
        out_specs=(hbm,) * 5,
        scratch_shapes=[dma((5,))],
    )(*outs[:5])
    return tuple(stored[:4]) + (stored[4].reshape(contract_dual.shape), outs[5])


def solution(mesh):
    cells = P(("groups", "hour"), "seg", "pipe")
    contracts = P(("groups", "hour"), "seg", "pipe", None)
    return jax.shard_map(
        on_device,
        mesh=mesh,
        in_specs=(
            cells, cells, cells, cells, contracts, cells, cells, contracts,
            P(), P("seg", ("groups", "pipe")), P("groups"), P(("groups", "hour"), None),
        ),
        out_specs=(cells, cells, cells, cells, contracts, P("groups")),
        check_vma=False,
    )
```

```python
import functools

import jax
import jax.numpy as jnp
from jax import lax
from jax.experimental import pallas as pl
from jax.experimental.pallas import tpu as pltpu
from jax.sharding import PartitionSpec as P

ITERS = 2
FLOW_CAP = 1.5
PACK_CAP = 2.5
STEP_SCALE = 0.25
NORM_EPS = 1e-06
LANES = 128
PIECES = 3


def pieces_of(values):
    parts = []
    rest = values
    for _ in range(PIECES):
        part = rest.astype(jnp.bfloat16)
        rest = rest - part.astype(jnp.float32)
        parts.append(part.astype(jnp.float32))
    return jnp.concatenate(parts, axis=0).astype(jnp.bfloat16)


def joined(stacked, rows):
    total = stacked[(PIECES - 1) * rows :]
    for piece in range(PIECES - 2, -1, -1):
        total = total + stacked[piece * rows : (piece + 1) * rows]
    return total


def folded(cells):
    rows, columns = cells.shape
    total = None
    for row in range(0, rows, 8):
        for column in range(0, columns, LANES):
            block = cells[row : row + 8, column : column + LANES]
            total = block if total is None else total + block
    return total


def kernel(
    sizes,
    table_ref,
    flow_in, pack_in, mass_in, mom_in, dual_in, cost_in, inj_in, target_in, class_in, match_in, map_in,
    flow_out, pack_out, mass_out, mom_out, dual_out, weight_out,
    flow, pack, mass, mom, dual, cost, inj, target, classes, match, cmap,
    fric, flow_bar, pack_bar, onehot_c, onehot_m,
    row_send, row_recv, hour_recv, sum_send, sum_recv, dual_recv, norm_send, norm_recv,
    in_sem, out_sem, row_ss, row_rs, hour_ss, hour_rs, sum_ss, sum_rs, dual_ss, dual_rs, norm_ss, norm_rs,
):
    pipes, hours, segs, H, S, W, C, R, T = sizes
    share = C / T
    peers = pipes * hours * segs
    me_p, me_h, me_s = lax.axis_index("pipe"), lax.axis_index("hour"), lax.axis_index("seg")
    me = (me_p * hours + me_h) * segs + me_s
    other_s = lax.rem(me_s + 1, segs)
    first_half, last_half = me_s == 0, me_s == segs - 1
    first_hour, last_hour = me_h == 0, me_h == hours - 1

    def load(index, source, place):
        copy = pltpu.make_async_copy(source, place, in_sem.at[index])
        copy.start()
        return copy

    get_mass = load(0, mass_in, mass.at[0])
    get_mom = load(1, mom_in, mom.at[0])
    get_dual = load(2, dual_in, dual.at[0])
    get_match = load(3, match_in, match)
    get_map = load(4, map_in, cmap)
    get_class = load(5, class_in, classes)
    get_flow = load(6, flow_in, flow.at[0])
    get_pack = load(7, pack_in, pack.at[0])
    get_cost = load(8, cost_in, cost)
    get_inj = load(9, inj_in, inj)
    get_target = load(10, target_in, target)

    def peer(step):
        dp, rest = step // (hours * segs), step % (hours * segs)
        return {
            "pipe": lax.rem(me_p + dp, pipes),
            "hour": lax.rem(me_h + rest // segs, hours),
            "seg": lax.rem(me_s + rest % segs, segs),
        }

    def each_peer(act):
        if peers <= 32:
            for step in range(1, peers):
                act(step)
        else:
            def body(step, carry):
                act(step)
                return carry
            lax.fori_loop(1, peers, body, 0)

    barrier = pltpu.get_barrier_semaphore()

    def greet(step):
        pl.semaphore_signal(barrier, inc=1, device_id=peer(step), device_id_type=pl.DeviceIdType.MESH)

    each_peer(greet)

    sent = []

    def remote(source, place, send_sem, recv_sem, where):
        copy = pltpu.make_async_remote_copy(
            src_ref=source, dst_ref=place, send_sem=send_sem, recv_sem=recv_sem,
            device_id=where, device_id_type=pl.DeviceIdType.MESH,
        )
        copy.start()
        sent.append(copy)
        return copy

    def send_rows(turn):
        return [
            remote(
                row_send.at[turn], row_recv.at[turn, me_p], row_ss.at[turn, step], row_rs.at[turn, step],
                {"pipe": lax.rem(me_p + step, pipes), "seg": other_s},
            )
            for step in range(pipes)
        ]

    def send_duals(it):
        dual_recv[it, me_p] = dual[it]
        return [
            remote(
                dual.at[it], dual_recv.at[it, me_p], dual_ss.at[it, step], dual_rs.at[it, step],
                {"pipe": lax.rem(me_p + step, pipes)},
            )
            for step in range(1, pipes)
        ]

    def send_sums(it):
        return [
            remote(
                sum_send.at[it, lax.rem(me_p + step, pipes)], sum_recv.at[it, me_p],
                sum_ss.at[it, step], sum_rs.at[it, step],
                {"pipe": lax.rem(me_p + step, pipes)},
            )
            for step in range(1, pipes)
        ]

    def norm_copy(it, step):
        return pltpu.make_async_remote_copy(
            src_ref=norm_send.at[it], dst_ref=norm_recv.at[it, me],
            send_sem=norm_ss.at[it, step], recv_sem=norm_rs.at[it, step],
            device_id=peer(step), device_id_type=pl.DeviceIdType.MESH,
        )

    def fill_dual_rows(it, turn):
        for h in range(H):
            row_send[turn, h : h + 1, :] = mass[it, h, 0:1, :]
            row_send[turn, H + h : H + h + 1, :] = mom[it, h, S - 1 : S, :]

    def send_dual_halo(it, turn):
        rows = send_rows(turn)
        layer = remote(
            mass.at[it, 0], hour_recv.at[turn], hour_ss.at[turn], hour_rs.at[turn],
            {"hour": lax.rem(me_h + hours - 1, hours)},
        )
        return rows + [layer]

    get_mass.wait()
    get_mom.wait()
    fill_dual_rows(0, 0)
    get_dual.wait()
    pl.semaphore_wait(barrier, peers - 1)
    waiting_duals = send_duals(0)
    waiting_halo = send_dual_halo(0, 0)

    get_map.wait()
    start = pl.multiple_of(me_p * W, LANES)
    own_map = cmap[:, pl.ds(start, W)]
    class_rows = lax.broadcasted_iota(jnp.int32, (C, W), 0)
    for h in range(H):
        onehot_c[h] = jnp.where(own_map[h : h + 1, :] == class_rows, 1.0, 0.0).astype(jnp.bfloat16)
    get_match.wait()

    @pl.when(first_half)
    def _():
        wanted = match[:, pl.ds(start, W)]
        rows = lax.broadcasted_iota(jnp.int32, (LANES, W), 0)
        for block in range(0, T, LANES):
            hit = wanted == rows + block
            onehot_m[block : block + LANES, :] = jnp.where(hit, 1.0, 0.0).astype(jnp.bfloat16)

    @pl.when(jnp.logical_not(first_half))
    def _():
        columns = lax.broadcasted_iota(jnp.int32, (LANES, W), 1).astype(jnp.float32)
        columns = columns + start.astype(jnp.float32)
        for block in range(0, T, LANES):
            line = match[:, block : block + LANES].astype(jnp.float32)
            upright = jnp.transpose(jnp.broadcast_to(line, (LANES, LANES)))
            hit = jnp.concatenate([upright] * (W // LANES), axis=1) == columns
            onehot_m[block : block + LANES, :] = jnp.where(hit, 1.0, 0.0).astype(jnp.bfloat16)

    get_class.wait()
    kinds = classes[...]
    level = jnp.zeros((S, W), jnp.float32)
    for kind in range(table_ref.shape[0]):
        level = jnp.where(kinds == kind, table_ref[kind], level)
    fric[...] = level

    def matched_rows(turn):
        line = jnp.concatenate([row_recv[turn, block] for block in range(pipes)], axis=1)
        found = jnp.dot(pieces_of(line), onehot_m[...], preferred_element_type=jnp.float32)
        return joined(found, 2 * H)

    seg_at = lax.broadcasted_iota(jnp.int32, (S, W), 0)
    top, bottom = seg_at == 0, seg_at == S - 1
    get_flow.wait()
    get_pack.wait()
    get_cost.wait()

    outgoing = []

    def put(index, source, place):
        copy = pltpu.make_async_copy(source, place, out_sem.at[index])
        copy.start()
        outgoing.append(copy)

    weight = None
    for it in range(ITERS):
        turn = 2 * it
        for copy in waiting_halo:
            copy.wait_recv()
        found = matched_rows(turn)
        near = row_recv[turn, me_p]
        next_row = jnp.where(first_half, near, found)
        before_row = jnp.where(first_half, 0.0, near)
        for copy in waiting_duals:
            copy.wait_recv()
        spreads = []
        for h in range(H):
            held = jnp.concatenate([dual_recv[it, block, h] for block in range(pipes)], axis=0)
            spreads.append(
                joined(jnp.dot(pieces_of(held), onehot_c[h], preferred_element_type=jnp.float32), S)
            )
        if it == 0:
            primal_step, dual_step = STEP_SCALE, STEP_SCALE
        else:
            weight = finish_norms(it - 1, weight)
            primal_step, dual_step = STEP_SCALE / weight, STEP_SCALE * weight
        primal_sq = jnp.zeros((S, W), jnp.float32)
        for h in range(H):
            m, r = mass[it, h], mom[it, h]
            later = mass[it, h + 1] if h < H - 1 else jnp.where(last_hour, 0.0, hour_recv[turn])
            next_seg = jnp.where(bottom, next_row[h : h + 1], pltpu.roll(m, S - 1, 0))
            before = jnp.where(top, before_row[H + h : H + h + 1], pltpu.roll(r, 1, 0))
            grad_flow = m - next_seg + fric[...] * r
            grad_pack = m - later - r + before + share * spreads[h]
            f, q = flow[it, h], pack[it, h]
            flow_next = jnp.clip(f - primal_step * (cost[h] - grad_flow), -FLOW_CAP, FLOW_CAP)
            pack_next = jnp.clip(q + primal_step * grad_pack, 0.0, PACK_CAP)
            flow[it + 1, h] = flow_next
            pack[it + 1, h] = pack_next
            fb, pb = 2.0 * flow_next - f, 2.0 * pack_next - q
            flow_bar[it, h] = fb
            pack_bar[it, h] = pb
            row_send[turn + 1, h : h + 1, :] = fb[S - 1 : S]
            row_send[turn + 1, H + h : H + h + 1, :] = pb[0:1]
            primal_sq = primal_sq + (flow_next - f) ** 2 + (pack_next - q) ** 2
            partial = joined(
                lax.dot_general(
                    pieces_of(pb), onehot_c[h], (((1,), (1,)), ((), ())),
                    preferred_element_type=jnp.float32,
                ),
                S,
            )
            for block in range(pipes):
                sum_send[it, block, h] = partial[block * R : (block + 1) * R]
        waiting_sums = send_sums(it)
        waiting_halo = send_rows(turn + 1)
        waiting_halo.append(
            remote(
                pack_bar.at[it, H - 1], hour_recv.at[turn + 1], hour_ss.at[turn + 1], hour_rs.at[turn + 1],
                {"hour": lax.rem(me_h + 1, hours)},
            )
        )
        if it == ITERS - 1:
            put(0, flow.at[ITERS], flow_out)
            put(1, pack.at[ITERS], pack_out)
        primal_block = folded(primal_sq)
        sum_recv[it, me_p] = sum_send[it, me_p]
        if it == 0:
            get_inj.wait()
            get_target.wait()
        for copy in waiting_halo:
            copy.wait_recv()
        found = matched_rows(turn + 1)
        near = row_recv[turn + 1, me_p]
        first_row = jnp.where(first_half, found, near)
        after_row = jnp.where(last_half, 0.0, near)
        dual_sq = jnp.zeros((S, W), jnp.float32)
        for h in range(H):
            fb, pb = flow_bar[it, h], pack_bar[it, h]
            m, r = mass[it, h], mom[it, h]
            earlier = pack_bar[it, h - 1] if h > 0 else jnp.where(first_hour, 0.0, hour_recv[turn + 1])
            upstream = jnp.where(top, first_row[h : h + 1], pltpu.roll(fb, 1, 0))
            after = jnp.where(bottom, after_row[H + h : H + h + 1], pltpu.roll(pb, S - 1, 0))
            mass_next = m + dual_step * (inj[h] - (pb - earlier + fb - upstream))
            mom_next = r - dual_step * (fric[...] * fb - (pb - after))
            mass[it + 1, h] = mass_next
            mom[it + 1, h] = mom_next
            dual_sq = dual_sq + (mass_next - m) ** 2 + (mom_next - r) ** 2
        if it < ITERS - 1:
            fill_dual_rows(it + 1, turn + 2)
            waiting_halo = send_dual_halo(it + 1, turn + 2)
        else:
            put(2, mass.at[ITERS], mass_out)
            put(3, mom.at[ITERS], mom_out)
        dual_block = folded(dual_sq)
        for copy in waiting_sums:
            copy.wait_recv()
        totals = sum_recv[it, 0]
        for block in range(1, pipes):
            totals = totals + sum_recv[it, block]
        held = dual[it]
        dual_next = held + dual_step * (target[...] - share * totals)
        dual[it + 1] = dual_next
        if it < ITERS - 1:
            waiting_duals = send_duals(it + 1)
        else:
            put(4, dual.at[ITERS], dual_out)
        change = (dual_next - held) ** 2
        lines = jnp.sum(change, axis=0)
        if R % 8 == 0:
            dual_block = dual_block + folded(lines)
        else:
            spot = lax.broadcasted_iota(jnp.int32, (8, C), 0) == 0
            dual_block = dual_block + jnp.where(spot, jnp.sum(lines, axis=0, keepdims=True), 0.0)
        upper = lax.broadcasted_iota(jnp.int32, (8, LANES), 0) < 4
        both = jnp.where(
            upper, primal_block + pltpu.roll(primal_block, 4, 0), dual_block + pltpu.roll(dual_block, 4, 0)
        )
        norm_send[it] = both
        norm_recv[it, me] = both
        each_peer(lambda step: norm_copy(it, step).start())

        def finish_norms(it, weight):
            each_peer(lambda step: norm_copy(it, step).wait_recv())
            total = jnp.sum(norm_recv[it], axis=0)
            primal = jnp.sum(jnp.where(upper, total, 0.0), axis=(0, 1), keepdims=True)
            dual_all = jnp.sum(jnp.where(upper, 0.0, total), axis=(0, 1), keepdims=True)
            ratio = jnp.sqrt((dual_all + NORM_EPS) / (primal + NORM_EPS))
            return jnp.sqrt(ratio if weight is None else weight * ratio)

    weight = finish_norms(ITERS - 1, weight)
    weight_out[0] = jnp.sum(weight)
    for copy in sent:
        copy.wait_send()
    for it in range(ITERS):
        each_peer(lambda step: norm_copy(it, step).wait_send())
    for copy in outgoing:
        copy.wait()


def store_kernel(*refs):
    count = (len(refs) - 2) // 3
    sources, places, held = refs[:count], refs[count : 2 * count], refs[2 * count : 3 * count]
    in_sem, out_sem = refs[-2:]
    loads = [pltpu.make_async_copy(sources[i], held[i], in_sem.at[i]) for i in range(count)]
    stores = [pltpu.make_async_copy(held[i], places[i], out_sem.at[i]) for i in range(count)]
    for copy in loads:
        copy.start()
    for load, store in zip(loads, stores):
        load.wait()
        store.start()
    for copy in stores:
        copy.wait()


def on_device(
    segment_flow, linepack, mass_dual, momentum_dual, contract_dual, flow_cost, injection, contract_target,
    friction_table, friction_class, matching, contract_map,
):
    H, S, W = segment_flow.shape
    C = contract_dual.shape[3]
    R = contract_dual.shape[2]
    pipes, hours, segs = lax.axis_size("pipe"), lax.axis_size("hour"), lax.axis_size("seg")
    peers = pipes * hours * segs
    T = W * pipes
    f32, i32 = jnp.float32, jnp.int32
    anywhere = pl.BlockSpec(memory_space=pl.ANY)
    hbm = pl.BlockSpec(memory_space=pltpu.HBM)
    smem = pl.BlockSpec(memory_space=pltpu.SMEM)
    cells = jax.ShapeDtypeStruct((H, S, W), f32)
    turns = 2 * ITERS
    dma = pltpu.SemaphoreType.DMA
    outs = pl.pallas_call(
        functools.partial(kernel, (pipes, hours, segs, H, S, W, C, R, T)),
        out_shape=(cells,) * 4
        + (jax.ShapeDtypeStruct((H, R, C), f32), jax.ShapeDtypeStruct((1,), f32)),
        in_specs=[smem] + [hbm] * 11,
        out_specs=(anywhere,) * 5 + (smem,),
        scratch_shapes=[
            pltpu.VMEM((ITERS + 1, H, S, W), f32),
            pltpu.VMEM((ITERS + 1, H, S, W), f32),
            pltpu.VMEM((ITERS + 1, H, S, W), f32),
            pltpu.VMEM((ITERS + 1, H, S, W), f32),
            pltpu.VMEM((ITERS + 1, H, R, C), f32),
            pltpu.VMEM((H, S, W), f32),
            pltpu.VMEM((H, S, W), f32),
            pltpu.VMEM((H, R, C), f32),
            pltpu.VMEM((S, W), i32),
            pltpu.VMEM((1, T), i32),
            pltpu.VMEM((H, T), i32),
            pltpu.VMEM((S, W), f32),
            pltpu.VMEM((ITERS, H, S, W), f32),
            pltpu.VMEM((ITERS, H, S, W), f32),
            pltpu.VMEM((H, C, W), jnp.bfloat16),
            pltpu.VMEM((T, W), jnp.bfloat16),
            pltpu.VMEM((turns, 2 * H, W), f32),
            pltpu.VMEM((turns, pipes, 2 * H, W), f32),
            pltpu.VMEM((turns, S, W), f32),
            pltpu.VMEM((ITERS, pipes, H, R, C), f32),
            pltpu.VMEM((ITERS, pipes, H, R, C), f32),
            pltpu.VMEM((ITERS, pipes, H, R, C), f32),
            pltpu.VMEM((ITERS, 8, LANES), f32),
            pltpu.VMEM((ITERS, peers, 8, LANES), f32),
            dma((11,)),
            dma((5,)),
            dma((turns, pipes)),
            dma((turns, pipes)),
            dma((turns,)),
            dma((turns,)),
            dma((ITERS, pipes)),
            dma((ITERS, pipes)),
            dma((ITERS, pipes)),
            dma((ITERS, pipes)),
            dma((ITERS, peers)),
            dma((ITERS, peers)),
        ],
        compiler_params=pltpu.CompilerParams(
            collective_id=0, has_side_effects=True, vmem_limit_bytes=63 * 1024 * 1024
        ),
        cost_estimate=pl.CostEstimate(flops=10**8, bytes_accessed=2 * 10**6, transcendentals=0),
    )(
        friction_table, segment_flow, linepack, mass_dual, momentum_dual, contract_dual.reshape(H, R, C),
        flow_cost, injection, contract_target.reshape(H, R, C), friction_class, matching.reshape(1, T),
        contract_map,
    )
    stored = pl.pallas_call(
        store_kernel,
        out_shape=(cells,) * 4 + (jax.ShapeDtypeStruct((H, R, C), f32),),
        in_specs=[anywhere] * 5,
        out_specs=(hbm,) * 5,
        scratch_shapes=[pltpu.VMEM((H, S, W), f32)] * 4
        + [pltpu.VMEM((H, R, C), f32), dma((5,)), dma((5,))],
        compiler_params=pltpu.CompilerParams(vmem_limit_bytes=63 * 1024 * 1024),
    )(*outs[:5])
    return tuple(stored[:4]) + (stored[4].reshape(contract_dual.shape), outs[5])


def solution(mesh):
    cells = P(("groups", "hour"), "seg", "pipe")
    contracts = P(("groups", "hour"), "seg", "pipe", None)
    return jax.shard_map(
        on_device,
        mesh=mesh,
        in_specs=(
            cells, cells, cells, cells, contracts, cells, cells, contracts,
            P(), P("seg", ("groups", "pipe")), P("groups"), P(("groups", "hour"), None),
        ),
        out_specs=(cells, cells, cells, cells, contracts, P("groups")),
        check_vma=False,
    )
```

```python
import functools

import jax
import jax.numpy as jnp
from jax import lax
from jax.experimental import pallas as pl
from jax.experimental.pallas import tpu as pltpu
from jax.sharding import PartitionSpec as P

ITERS = 2
FLOW_CAP = 1.5
PACK_CAP = 2.5
STEP_SCALE = 0.25
NORM_EPS = 1e-06
LANES = 128
PIECES = 2


def pieces_of(values):
    parts = []
    rest = values
    for _ in range(PIECES):
        part = rest.astype(jnp.bfloat16)
        rest = rest - part.astype(jnp.float32)
        parts.append(part.astype(jnp.float32))
    return jnp.concatenate(parts, axis=0).astype(jnp.bfloat16)


def joined(stacked, rows):
    total = stacked[(PIECES - 1) * rows :]
    for piece in range(PIECES - 2, -1, -1):
        total = total + stacked[piece * rows : (piece + 1) * rows]
    return total


def folded(cells):
    rows, columns = cells.shape
    total = None
    for row in range(0, rows, 8):
        for column in range(0, columns, LANES):
            block = cells[row : row + 8, column : column + LANES]
            total = block if total is None else total + block
    return total


def kernel(
    sizes,
    table_ref,
    flow_in, pack_in, mass_in, mom_in, dual_in, cost_in, inj_in, target_in, class_in, match_in, map_in,
    flow_out, pack_out, mass_out, mom_out, dual_out, weight_out,
    flow, pack, mass, mom, dual, cost, inj, target, classes, match, cmap,
    fric, flow_bar, pack_bar, onehot_c, onehot_m,
    row_send, row_recv, hour_recv, sum_send, sum_recv, dual_recv, norm_send, norm_recv,
    in_sem, out_sem, row_ss, row_rs, hour_ss, hour_rs, sum_ss, sum_rs, dual_ss, dual_rs, norm_ss, norm_rs,
):
    pipes, hours, segs, H, S, W, C, R, T = sizes
    share = C / T
    peers = pipes * hours * segs
    me_p, me_h, me_s = lax.axis_index("pipe"), lax.axis_index("hour"), lax.axis_index("seg")
    me = (me_p * hours + me_h) * segs + me_s
    other_s = lax.rem(me_s + 1, segs)
    first_half, last_half = me_s == 0, me_s == segs - 1
    first_hour, last_hour = me_h == 0, me_h == hours - 1

    def load(index, source, place):
        copy = pltpu.make_async_copy(source, place, in_sem.at[index])
        copy.start()
        return copy

    get_mass = load(0, mass_in, mass.at[0])
    get_mom = load(1, mom_in, mom.at[0])
    get_dual = load(2, dual_in, dual.at[0])
    get_match = load(3, match_in, match)
    get_map = load(4, map_in, cmap)
    get_class = load(5, class_in, classes)
    get_flow = load(6, flow_in, flow.at[0])
    get_pack = load(7, pack_in, pack.at[0])
    get_cost = load(8, cost_in, cost)
    get_inj = load(9, inj_in, inj)
    get_target = load(10, target_in, target)

    def peer(step):
        dp, rest = step // (hours * segs), step % (hours * segs)
        return {
            "pipe": lax.rem(me_p + dp, pipes),
            "hour": lax.rem(me_h + rest // segs, hours),
            "seg": lax.rem(me_s + rest % segs, segs),
        }

    def each_peer(act):
        if peers <= 32:
            for step in range(1, peers):
                act(step)
        else:
            def body(step, carry):
                act(step)
                return carry
            lax.fori_loop(1, peers, body, 0)

    barrier = pltpu.get_barrier_semaphore()

    def greet(step):
        pl.semaphore_signal(barrier, inc=1, device_id=peer(step), device_id_type=pl.DeviceIdType.MESH)

    each_peer(greet)

    sent = []

    def remote(source, place, send_sem, recv_sem, where):
        copy = pltpu.make_async_remote_copy(
            src_ref=source, dst_ref=place, send_sem=send_sem, recv_sem=recv_sem,
            device_id=where, device_id_type=pl.DeviceIdType.MESH,
        )
        copy.start()
        sent.append(copy)
        return copy

    def send_rows(turn):
        return [
            remote(
                row_send.at[turn], row_recv.at[turn, me_p], row_ss.at[turn, step], row_rs.at[turn, step],
                {"pipe": lax.rem(me_p + step, pipes), "seg": other_s},
            )
            for step in range(pipes)
        ]

    def send_duals(it):
        dual_recv[it, me_p] = dual[it]
        return [
            remote(
                dual.at[it], dual_recv.at[it, me_p], dual_ss.at[it, step], dual_rs.at[it, step],
                {"pipe": lax.rem(me_p + step, pipes)},
            )
            for step in range(1, pipes)
        ]

    def send_sums(it):
        return [
            remote(
                sum_send.at[it, lax.rem(me_p + step, pipes)], sum_recv.at[it, me_p],
                sum_ss.at[it, step], sum_rs.at[it, step],
                {"pipe": lax.rem(me_p + step, pipes)},
            )
            for step in range(1, pipes)
        ]

    def norm_copy(it, step):
        return pltpu.make_async_remote_copy(
            src_ref=norm_send.at[it], dst_ref=norm_recv.at[it, me],
            send_sem=norm_ss.at[it, step], recv_sem=norm_rs.at[it, step],
            device_id=peer(step), device_id_type=pl.DeviceIdType.MESH,
        )

    def fill_dual_rows(it, turn):
        for h in range(H):
            row_send[turn, h : h + 1, :] = mass[it, h, 0:1, :]
            row_send[turn, H + h : H + h + 1, :] = mom[it, h, S - 1 : S, :]

    def send_dual_halo(it, turn):
        rows = send_rows(turn)
        layer = remote(
            mass.at[it, 0], hour_recv.at[turn], hour_ss.at[turn], hour_rs.at[turn],
            {"hour": lax.rem(me_h + hours - 1, hours)},
        )
        return rows + [layer]

    get_mass.wait()
    get_mom.wait()
    fill_dual_rows(0, 0)
    get_dual.wait()
    pl.semaphore_wait(barrier, peers - 1)
    waiting_duals = send_duals(0)
    waiting_halo = send_dual_halo(0, 0)

    get_map.wait()
    start = pl.multiple_of(me_p * W, LANES)
    own_map = cmap[:, pl.ds(start, W)]
    class_rows = lax.broadcasted_iota(jnp.int32, (C, W), 0)
    for h in range(H):
        onehot_c[h] = jnp.where(own_map[h : h + 1, :] == class_rows, 1.0, 0.0).astype(jnp.bfloat16)
    get_match.wait()

    @pl.when(first_half)
    def _():
        wanted = match[:, pl.ds(start, W)]
        rows = lax.broadcasted_iota(jnp.int32, (LANES, W), 0)
        for block in range(0, T, LANES):
            hit = wanted == rows + block
            onehot_m[block : block + LANES, :] = jnp.where(hit, 1.0, 0.0).astype(jnp.bfloat16)

    @pl.when(jnp.logical_not(first_half))
    def _():
        columns = lax.broadcasted_iota(jnp.int32, (LANES, W), 1).astype(jnp.float32)
        columns = columns + start.astype(jnp.float32)
        for block in range(0, T, LANES):
            line = match[:, block : block + LANES].astype(jnp.float32)
            upright = jnp.transpose(jnp.broadcast_to(line, (LANES, LANES)))
            hit = jnp.concatenate([upright] * (W // LANES), axis=1) == columns
            onehot_m[block : block + LANES, :] = jnp.where(hit, 1.0, 0.0).astype(jnp.bfloat16)

    get_class.wait()
    kinds = classes[...]
    level = jnp.zeros((S, W), jnp.float32)
    for kind in range(table_ref.shape[0]):
        level = jnp.where(kinds == kind, table_ref[kind], level)
    fric[...] = level

    def matched_rows(turn):
        line = jnp.concatenate([row_recv[turn, block] for block in range(pipes)], axis=1)
        found = jnp.dot(pieces_of(line), onehot_m[...], preferred_element_type=jnp.float32)
        return joined(found, 2 * H)

    seg_at = lax.broadcasted_iota(jnp.int32, (S, W), 0)
    top, bottom = seg_at == 0, seg_at == S - 1
    get_flow.wait()
    get_pack.wait()
    get_cost.wait()

    outgoing = []

    def put(index, source, place):
        copy = pltpu.make_async_copy(source, place, out_sem.at[index])
        copy.start()
        outgoing.append(copy)

    weight = None
    for it in range(ITERS):
        turn = 2 * it
        for copy in waiting_halo:
            copy.wait_recv()
        found = matched_rows(turn)
        near = row_recv[turn, me_p]
        next_row = jnp.where(first_half, near, found)
        before_row = jnp.where(first_half, 0.0, near)
        for copy in waiting_duals:
            copy.wait_recv()
        spreads = []
        for h in range(H):
            held = jnp.concatenate([dual_recv[it, block, h] for block in range(pipes)], axis=0)
            spreads.append(
                joined(jnp.dot(pieces_of(held), onehot_c[h], preferred_element_type=jnp.float32), S)
            )
        if it == 0:
            primal_step, dual_step = STEP_SCALE, STEP_SCALE
        else:
            weight = finish_norms(it - 1, weight)
            primal_step, dual_step = STEP_SCALE / weight, STEP_SCALE * weight
        primal_sq = jnp.zeros((S, W), jnp.float32)
        for h in range(H):
            m, r = mass[it, h], mom[it, h]
            later = mass[it, h + 1] if h < H - 1 else jnp.where(last_hour, 0.0, hour_recv[turn])
            next_seg = jnp.where(bottom, next_row[h : h + 1], pltpu.roll(m, S - 1, 0))
            before = jnp.where(top, before_row[H + h : H + h + 1], pltpu.roll(r, 1, 0))
            grad_flow = m - next_seg + fric[...] * r
            grad_pack = m - later - r + before + share * spreads[h]
            f, q = flow[it, h], pack[it, h]
            flow_next = jnp.clip(f - primal_step * (cost[h] - grad_flow), -FLOW_CAP, FLOW_CAP)
            pack_next = jnp.clip(q + primal_step * grad_pack, 0.0, PACK_CAP)
            flow[it + 1, h] = flow_next
            pack[it + 1, h] = pack_next
            fb, pb = 2.0 * flow_next - f, 2.0 * pack_next - q
            flow_bar[it, h] = fb
            pack_bar[it, h] = pb
            row_send[turn + 1, h : h + 1, :] = fb[S - 1 : S]
            row_send[turn + 1, H + h : H + h + 1, :] = pb[0:1]
            primal_sq = primal_sq + (flow_next - f) ** 2 + (pack_next - q) ** 2
            partial = joined(
                lax.dot_general(
                    pieces_of(pb), onehot_c[h], (((1,), (1,)), ((), ())),
                    preferred_element_type=jnp.float32,
                ),
                S,
            )
            for block in range(pipes):
                sum_send[it, block, h] = partial[block * R : (block + 1) * R]
        waiting_sums = send_sums(it)
        waiting_halo = send_rows(turn + 1)
        waiting_halo.append(
            remote(
                pack_bar.at[it, H - 1], hour_recv.at[turn + 1], hour_ss.at[turn + 1], hour_rs.at[turn + 1],
                {"hour": lax.rem(me_h + 1, hours)},
            )
        )
        if it == ITERS - 1:
            put(0, flow.at[ITERS], flow_out)
            put(1, pack.at[ITERS], pack_out)
        primal_block = folded(primal_sq)
        sum_recv[it, me_p] = sum_send[it, me_p]
        if it == 0:
            get_inj.wait()
            get_target.wait()
        for copy in waiting_halo:
            copy.wait_recv()
        found = matched_rows(turn + 1)
        near = row_recv[turn + 1, me_p]
        first_row = jnp.where(first_half, found, near)
        after_row = jnp.where(last_half, 0.0, near)
        dual_sq = jnp.zeros((S, W), jnp.float32)
        for h in range(H):
            fb, pb = flow_bar[it, h], pack_bar[it, h]
            m, r = mass[it, h], mom[it, h]
            earlier = pack_bar[it, h - 1] if h > 0 else jnp.where(first_hour, 0.0, hour_recv[turn + 1])
            upstream = jnp.where(top, first_row[h : h + 1], pltpu.roll(fb, 1, 0))
            after = jnp.where(bottom, after_row[H + h : H + h + 1], pltpu.roll(pb, S - 1, 0))
            mass_next = m + dual_step * (inj[h] - (pb - earlier + fb - upstream))
            mom_next = r - dual_step * (fric[...] * fb - (pb - after))
            mass[it + 1, h] = mass_next
            mom[it + 1, h] = mom_next
            dual_sq = dual_sq + (mass_next - m) ** 2 + (mom_next - r) ** 2
        if it < ITERS - 1:
            fill_dual_rows(it + 1, turn + 2)
            waiting_halo = send_dual_halo(it + 1, turn + 2)
        else:
            put(2, mass.at[ITERS], mass_out)
            put(3, mom.at[ITERS], mom_out)
        dual_block = folded(dual_sq)
        for copy in waiting_sums:
            copy.wait_recv()
        totals = sum_recv[it, 0]
        for block in range(1, pipes):
            totals = totals + sum_recv[it, block]
        held = dual[it]
        dual_next = held + dual_step * (target[...] - share * totals)
        dual[it + 1] = dual_next
        if it < ITERS - 1:
            waiting_duals = send_duals(it + 1)
        else:
            put(4, dual.at[ITERS], dual_out)
        change = (dual_next - held) ** 2
        lines = jnp.sum(change, axis=0)
        if R % 8 == 0:
            dual_block = dual_block + folded(lines)
        else:
            spot = lax.broadcasted_iota(jnp.int32, (8, C), 0) == 0
            dual_block = dual_block + jnp.where(spot, jnp.sum(lines, axis=0, keepdims=True), 0.0)
        upper = lax.broadcasted_iota(jnp.int32, (8, LANES), 0) < 4
        both = jnp.where(
            upper, primal_block + pltpu.roll(primal_block, 4, 0), dual_block + pltpu.roll(dual_block, 4, 0)
        )
        norm_send[it] = both
        norm_recv[it, me] = both
        each_peer(lambda step: norm_copy(it, step).start())

        def finish_norms(it, weight):
            each_peer(lambda step: norm_copy(it, step).wait_recv())
            total = jnp.sum(norm_recv[it], axis=0)
            primal = jnp.sum(jnp.where(upper, total, 0.0), axis=(0, 1), keepdims=True)
            dual_all = jnp.sum(jnp.where(upper, 0.0, total), axis=(0, 1), keepdims=True)
            ratio = jnp.sqrt((dual_all + NORM_EPS) / (primal + NORM_EPS))
            return jnp.sqrt(ratio if weight is None else weight * ratio)

    weight = finish_norms(ITERS - 1, weight)
    weight_out[0] = jnp.sum(weight)
    for copy in sent:
        copy.wait_send()
    for it in range(ITERS):
        each_peer(lambda step: norm_copy(it, step).wait_send())
    for copy in outgoing:
        copy.wait()


def store_kernel(*refs):
    count = (len(refs) - 2) // 3
    sources, places, held = refs[:count], refs[count : 2 * count], refs[2 * count : 3 * count]
    in_sem, out_sem = refs[-2:]
    loads = [pltpu.make_async_copy(sources[i], held[i], in_sem.at[i]) for i in range(count)]
    stores = [pltpu.make_async_copy(held[i], places[i], out_sem.at[i]) for i in range(count)]
    for copy in loads:
        copy.start()
    for load, store in zip(loads, stores):
        load.wait()
        store.start()
    for copy in stores:
        copy.wait()


def on_device(
    segment_flow, linepack, mass_dual, momentum_dual, contract_dual, flow_cost, injection, contract_target,
    friction_table, friction_class, matching, contract_map,
):
    H, S, W = segment_flow.shape
    C = contract_dual.shape[3]
    R = contract_dual.shape[2]
    pipes, hours, segs = lax.axis_size("pipe"), lax.axis_size("hour"), lax.axis_size("seg")
    peers = pipes * hours * segs
    T = W * pipes
    f32, i32 = jnp.float32, jnp.int32
    anywhere = pl.BlockSpec(memory_space=pl.ANY)
    hbm = pl.BlockSpec(memory_space=pltpu.HBM)
    smem = pl.BlockSpec(memory_space=pltpu.SMEM)
    cells = jax.ShapeDtypeStruct((H, S, W), f32)
    turns = 2 * ITERS
    dma = pltpu.SemaphoreType.DMA
    outs = pl.pallas_call(
        functools.partial(kernel, (pipes, hours, segs, H, S, W, C, R, T)),
        out_shape=(cells,) * 4
        + (jax.ShapeDtypeStruct((H, R, C), f32), jax.ShapeDtypeStruct((1,), f32)),
        in_specs=[smem] + [hbm] * 11,
        out_specs=(anywhere,) * 5 + (smem,),
        scratch_shapes=[
            pltpu.VMEM((ITERS + 1, H, S, W), f32),
            pltpu.VMEM((ITERS + 1, H, S, W), f32),
            pltpu.VMEM((ITERS + 1, H, S, W), f32),
            pltpu.VMEM((ITERS + 1, H, S, W), f32),
            pltpu.VMEM((ITERS + 1, H, R, C), f32),
            pltpu.VMEM((H, S, W), f32),
            pltpu.VMEM((H, S, W), f32),
            pltpu.VMEM((H, R, C), f32),
            pltpu.VMEM((S, W), i32),
            pltpu.VMEM((1, T), i32),
            pltpu.VMEM((H, T), i32),
            pltpu.VMEM((S, W), f32),
            pltpu.VMEM((ITERS, H, S, W), f32),
            pltpu.VMEM((ITERS, H, S, W), f32),
            pltpu.VMEM((H, C, W), jnp.bfloat16),
            pltpu.VMEM((T, W), jnp.bfloat16),
            pltpu.VMEM((turns, 2 * H, W), f32),
            pltpu.VMEM((turns, pipes, 2 * H, W), f32),
            pltpu.VMEM((turns, S, W), f32),
            pltpu.VMEM((ITERS, pipes, H, R, C), f32),
            pltpu.VMEM((ITERS, pipes, H, R, C), f32),
            pltpu.VMEM((ITERS, pipes, H, R, C), f32),
            pltpu.VMEM((ITERS, 8, LANES), f32),
            pltpu.VMEM((ITERS, peers, 8, LANES), f32),
            dma((11,)),
            dma((5,)),
            dma((turns, pipes)),
            dma((turns, pipes)),
            dma((turns,)),
            dma((turns,)),
            dma((ITERS, pipes)),
            dma((ITERS, pipes)),
            dma((ITERS, pipes)),
            dma((ITERS, pipes)),
            dma((ITERS, peers)),
            dma((ITERS, peers)),
        ],
        compiler_params=pltpu.CompilerParams(
            collective_id=0, has_side_effects=True, vmem_limit_bytes=63 * 1024 * 1024
        ),
        cost_estimate=pl.CostEstimate(flops=10**8, bytes_accessed=2 * 10**6, transcendentals=0),
    )(
        friction_table, segment_flow, linepack, mass_dual, momentum_dual, contract_dual.reshape(H, R, C),
        flow_cost, injection, contract_target.reshape(H, R, C), friction_class, matching.reshape(1, T),
        contract_map,
    )
    stored = pl.pallas_call(
        store_kernel,
        out_shape=(cells,) * 4 + (jax.ShapeDtypeStruct((H, R, C), f32),),
        in_specs=[anywhere] * 5,
        out_specs=(hbm,) * 5,
        scratch_shapes=[pltpu.VMEM((H, S, W), f32)] * 4
        + [pltpu.VMEM((H, R, C), f32), dma((5,)), dma((5,))],
        compiler_params=pltpu.CompilerParams(vmem_limit_bytes=63 * 1024 * 1024),
    )(*outs[:5])
    return tuple(stored[:4]) + (stored[4].reshape(contract_dual.shape), outs[5])


def solution(mesh):
    cells = P(("groups", "hour"), "seg", "pipe")
    contracts = P(("groups", "hour"), "seg", "pipe", None)
    return jax.shard_map(
        on_device,
        mesh=mesh,
        in_specs=(
            cells, cells, cells, cells, contracts, cells, cells, contracts,
            P(), P("seg", ("groups", "pipe")), P("groups"), P(("groups", "hour"), None),
        ),
        out_specs=(cells, cells, cells, cells, contracts, P("groups")),
        check_vma=False,
    )
```

```python
import functools

import jax
import jax.numpy as jnp
from jax import lax
from jax.experimental import pallas as pl
from jax.experimental.pallas import tpu as pltpu
from jax.sharding import PartitionSpec as P

ITERS = 2
FLOW_CAP = 1.5
PACK_CAP = 2.5
STEP_SCALE = 0.25
NORM_EPS = 1e-06
LANES = 128
PIECES = 3


def pieces_of(values):
    parts = []
    rest = values
    for _ in range(PIECES):
        part = rest.astype(jnp.bfloat16)
        rest = rest - part.astype(jnp.float32)
        parts.append(part.astype(jnp.float32))
    return jnp.concatenate(parts, axis=0).astype(jnp.bfloat16)


def joined(stacked, rows):
    total = stacked[(PIECES - 1) * rows :]
    for piece in range(PIECES - 2, -1, -1):
        total = total + stacked[piece * rows : (piece + 1) * rows]
    return total


def folded(cells):
    rows, columns = cells.shape
    total = None
    for row in range(0, rows, 8):
        for column in range(0, columns, LANES):
            block = cells[row : row + 8, column : column + LANES]
            total = block if total is None else total + block
    return total


def kernel(
    sizes,
    table_ref,
    flow_in, pack_in, mass_in, mom_in, dual_in, cost_in, inj_in, target_in, class_in, match_in, map_in,
    flow_out, pack_out, mass_out, mom_out, dual_out, weight_out,
    flow, pack, mass, mom, dual, cost, inj, target, classes, match, cmap,
    fric, flow_bar, pack_bar, onehot_c, onehot_m,
    row_send, row_recv, hour_recv, sum_send, sum_recv, dual_recv, norm_send, norm_recv,
    in_sem, out_sem, row_ss, row_rs, hour_ss, hour_rs, sum_ss, sum_rs, dual_ss, dual_rs, norm_ss, norm_rs,
):
    pipes, hours, segs, H, S, W, C, R, T = sizes
    share = C / T
    peers = pipes * hours * segs
    me_p, me_h, me_s = lax.axis_index("pipe"), lax.axis_index("hour"), lax.axis_index("seg")
    me = (me_p * hours + me_h) * segs + me_s
    other_s = lax.rem(me_s + 1, segs)
    first_half, last_half = me_s == 0, me_s == segs - 1
    first_hour, last_hour = me_h == 0, me_h == hours - 1

    def load(index, source, place):
        copy = pltpu.make_async_copy(source, place, in_sem.at[index])
        copy.start()
        return copy

    get_mass = load(0, mass_in, mass.at[0])
    get_mom = load(1, mom_in, mom.at[0])
    get_dual = load(2, dual_in, dual.at[0])
    get_match = load(3, match_in, match)
    get_map = load(4, map_in, cmap)
    get_class = load(5, class_in, classes)
    get_flow = load(6, flow_in, flow.at[0])
    get_pack = load(7, pack_in, pack.at[0])
    get_cost = load(8, cost_in, cost)
    get_inj = load(9, inj_in, inj)
    get_target = load(10, target_in, target)

    def peer(step):
        dp, rest = step // (hours * segs), step % (hours * segs)
        return {
            "pipe": lax.rem(me_p + dp, pipes),
            "hour": lax.rem(me_h + rest // segs, hours),
            "seg": lax.rem(me_s + rest % segs, segs),
        }

    def each_peer(act):
        if peers <= 32:
            for step in range(1, peers):
                act(step)
        else:
            def body(step, carry):
                act(step)
                return carry
            lax.fori_loop(1, peers, body, 0)

    barrier = pltpu.get_barrier_semaphore()

    def greet(step):
        pl.semaphore_signal(barrier, inc=1, device_id=peer(step), device_id_type=pl.DeviceIdType.MESH)

    each_peer(greet)

    sent = []

    def remote(source, place, send_sem, recv_sem, where):
        copy = pltpu.make_async_remote_copy(
            src_ref=source, dst_ref=place, send_sem=send_sem, recv_sem=recv_sem,
            device_id=where, device_id_type=pl.DeviceIdType.MESH,
        )
        copy.start()
        sent.append(copy)
        return copy

    def send_rows(turn):
        return [
            remote(
                row_send.at[turn], row_recv.at[turn, me_p], row_ss.at[turn, step], row_rs.at[turn, step],
                {"pipe": lax.rem(me_p + step, pipes), "seg": other_s},
            )
            for step in range(pipes)
        ]

    def send_duals(it):
        dual_recv[it, me_p] = dual[it]
        return [
            remote(
                dual.at[it], dual_recv.at[it, me_p], dual_ss.at[it, step], dual_rs.at[it, step],
                {"pipe": lax.rem(me_p + step, pipes)},
            )
            for step in range(1, pipes)
        ]

    def send_sums(it):
        return [
            remote(
                sum_send.at[it, lax.rem(me_p + step, pipes)], sum_recv.at[it, me_p],
                sum_ss.at[it, step], sum_rs.at[it, step],
                {"pipe": lax.rem(me_p + step, pipes)},
            )
            for step in range(1, pipes)
        ]

    def norm_copy(it, step):
        return pltpu.make_async_remote_copy(
            src_ref=norm_send.at[it], dst_ref=norm_recv.at[it, me],
            send_sem=norm_ss.at[it, step], recv_sem=norm_rs.at[it, step],
            device_id=peer(step), device_id_type=pl.DeviceIdType.MESH,
        )

    def fill_dual_rows(it, turn):
        for h in range(H):
            row_send[turn, h : h + 1, :] = mass[it, h, 0:1, :]
            row_send[turn, H + h : H + h + 1, :] = mom[it, h, S - 1 : S, :]

    def send_dual_halo(it, turn):
        rows = send_rows(turn)
        layer = remote(
            mass.at[it, 0], hour_recv.at[turn], hour_ss.at[turn], hour_rs.at[turn],
            {"hour": lax.rem(me_h + hours - 1, hours)},
        )
        return rows + [layer]

    get_mass.wait()
    get_mom.wait()
    fill_dual_rows(0, 0)
    get_dual.wait()
    get_map.wait()
    start = pl.multiple_of(me_p * W, LANES)
    own_map = cmap[:, pl.ds(start, W)]
    class_rows = lax.broadcasted_iota(jnp.int32, (C, W), 0)
    for h in range(H):
        onehot_c[h] = jnp.where(own_map[h : h + 1, :] == class_rows, 1.0, 0.0).astype(jnp.bfloat16)
    get_class.wait()
    kinds = classes[...]
    level = jnp.zeros((S, W), jnp.float32)
    for kind in range(table_ref.shape[0]):
        level = jnp.where(kinds == kind, table_ref[kind], level)
    fric[...] = level
    pl.semaphore_wait(barrier, peers - 1)
    waiting_duals = send_duals(0)
    waiting_halo = send_dual_halo(0, 0)

    get_match.wait()

    @pl.when(first_half)
    def _():
        wanted = match[:, pl.ds(start, W)]
        rows = lax.broadcasted_iota(jnp.int32, (LANES, W), 0)
        for block in range(0, T, LANES):
            hit = wanted == rows + block
            onehot_m[block : block + LANES, :] = jnp.where(hit, 1.0, 0.0).astype(jnp.bfloat16)

    @pl.when(jnp.logical_not(first_half))
    def _():
        columns = lax.broadcasted_iota(jnp.int32, (LANES, W), 1).astype(jnp.float32)
        columns = columns + start.astype(jnp.float32)
        for block in range(0, T, LANES):
            line = match[:, block : block + LANES].astype(jnp.float32)
            upright = jnp.transpose(jnp.broadcast_to(line, (LANES, LANES)))
            hit = jnp.concatenate([upright] * (W // LANES), axis=1) == columns
            onehot_m[block : block + LANES, :] = jnp.where(hit, 1.0, 0.0).astype(jnp.bfloat16)

    def matched_rows(turn):
        line = jnp.concatenate([row_recv[turn, block] for block in range(pipes)], axis=1)
        found = jnp.dot(pieces_of(line), onehot_m[...], preferred_element_type=jnp.float32)
        return joined(found, 2 * H)

    seg_at = lax.broadcasted_iota(jnp.int32, (S, W), 0)
    top, bottom = seg_at == 0, seg_at == S - 1
    get_flow.wait()
    get_pack.wait()
    get_cost.wait()

    outgoing = []

    def put(index, source, place):
        copy = pltpu.make_async_copy(source, place, out_sem.at[index])
        copy.start()
        outgoing.append(copy)

    weight = None
    for it in range(ITERS):
        turn = 2 * it
        for copy in waiting_halo:
            copy.wait_recv()
        found = matched_rows(turn)
        near = row_recv[turn, me_p]
        next_row = jnp.where(first_half, near, found)
        before_row = jnp.where(first_half, 0.0, near)
        for copy in waiting_duals:
            copy.wait_recv()
        spreads = []
        for h in range(H):
            held = jnp.concatenate([dual_recv[it, block, h] for block in range(pipes)], axis=0)
            spreads.append(
                joined(jnp.dot(pieces_of(held), onehot_c[h], preferred_element_type=jnp.float32), S)
            )
        if it == 0:
            primal_step, dual_step = STEP_SCALE, STEP_SCALE
        else:
            weight = finish_norms(it - 1, weight)
            primal_step, dual_step = STEP_SCALE / weight, STEP_SCALE * weight
        primal_sq = jnp.zeros((S, W), jnp.float32)
        for h in range(H):
            m, r = mass[it, h], mom[it, h]
            later = mass[it, h + 1] if h < H - 1 else jnp.where(last_hour, 0.0, hour_recv[turn])
            next_seg = jnp.where(bottom, next_row[h : h + 1], pltpu.roll(m, S - 1, 0))
            before = jnp.where(top, before_row[H + h : H + h + 1], pltpu.roll(r, 1, 0))
            grad_flow = m - next_seg + fric[...] * r
            grad_pack = m - later - r + before + share * spreads[h]
            f, q = flow[it, h], pack[it, h]
            flow_next = jnp.clip(f - primal_step * (cost[h] - grad_flow), -FLOW_CAP, FLOW_CAP)
            pack_next = jnp.clip(q + primal_step * grad_pack, 0.0, PACK_CAP)
            flow[it + 1, h] = flow_next
            pack[it + 1, h] = pack_next
            fb, pb = 2.0 * flow_next - f, 2.0 * pack_next - q
            flow_bar[it, h] = fb
            pack_bar[it, h] = pb
            row_send[turn + 1, h : h + 1, :] = fb[S - 1 : S]
            row_send[turn + 1, H + h : H + h + 1, :] = pb[0:1]
            primal_sq = primal_sq + (flow_next - f) ** 2 + (pack_next - q) ** 2
            partial = joined(
                lax.dot_general(
                    pieces_of(pb), onehot_c[h], (((1,), (1,)), ((), ())),
                    preferred_element_type=jnp.float32,
                ),
                S,
            )
            for block in range(pipes):
                sum_send[it, block, h] = partial[block * R : (block + 1) * R]
        waiting_sums = send_sums(it)
        waiting_halo = send_rows(turn + 1)
        waiting_halo.append(
            remote(
                pack_bar.at[it, H - 1], hour_recv.at[turn + 1], hour_ss.at[turn + 1], hour_rs.at[turn + 1],
                {"hour": lax.rem(me_h + 1, hours)},
            )
        )
        if it == ITERS - 1:
            put(0, flow.at[ITERS], flow_out)
            put(1, pack.at[ITERS], pack_out)
        primal_block = folded(primal_sq)
        sum_recv[it, me_p] = sum_send[it, me_p]
        if it == 0:
            get_inj.wait()
            get_target.wait()
        for copy in waiting_halo:
            copy.wait_recv()
        found = matched_rows(turn + 1)
        near = row_recv[turn + 1, me_p]
        first_row = jnp.where(first_half, found, near)
        after_row = jnp.where(last_half, 0.0, near)
        dual_sq = jnp.zeros((S, W), jnp.float32)
        for h in range(H):
            fb, pb = flow_bar[it, h], pack_bar[it, h]
            m, r = mass[it, h], mom[it, h]
            earlier = pack_bar[it, h - 1] if h > 0 else jnp.where(first_hour, 0.0, hour_recv[turn + 1])
            upstream = jnp.where(top, first_row[h : h + 1], pltpu.roll(fb, 1, 0))
            after = jnp.where(bottom, after_row[H + h : H + h + 1], pltpu.roll(pb, S - 1, 0))
            mass_next = m + dual_step * (inj[h] - (pb - earlier + fb - upstream))
            mom_next = r - dual_step * (fric[...] * fb - (pb - after))
            mass[it + 1, h] = mass_next
            mom[it + 1, h] = mom_next
            dual_sq = dual_sq + (mass_next - m) ** 2 + (mom_next - r) ** 2
        if it < ITERS - 1:
            fill_dual_rows(it + 1, turn + 2)
            waiting_halo = send_dual_halo(it + 1, turn + 2)
        else:
            put(2, mass.at[ITERS], mass_out)
            put(3, mom.at[ITERS], mom_out)
        dual_block = folded(dual_sq)
        for copy in waiting_sums:
            copy.wait_recv()
        totals = sum_recv[it, 0]
        for block in range(1, pipes):
            totals = totals + sum_recv[it, block]
        held = dual[it]
        dual_next = held + dual_step * (target[...] - share * totals)
        dual[it + 1] = dual_next
        if it < ITERS - 1:
            waiting_duals = send_duals(it + 1)
        else:
            put(4, dual.at[ITERS], dual_out)
        change = (dual_next - held) ** 2
        lines = jnp.sum(change, axis=0)
        if R % 8 == 0:
            dual_block = dual_block + folded(lines)
        else:
            spot = lax.broadcasted_iota(jnp.int32, (8, C), 0) == 0
            dual_block = dual_block + jnp.where(spot, jnp.sum(lines, axis=0, keepdims=True), 0.0)
        upper = lax.broadcasted_iota(jnp.int32, (8, LANES), 0) < 4
        both = jnp.where(
            upper, primal_block + pltpu.roll(primal_block, 4, 0), dual_block + pltpu.roll(dual_block, 4, 0)
        )
        norm_send[it] = both
        norm_recv[it, me] = both
        each_peer(lambda step: norm_copy(it, step).start())

        def finish_norms(it, weight):
            each_peer(lambda step: norm_copy(it, step).wait_recv())
            total = jnp.sum(norm_recv[it], axis=0)
            primal = jnp.sum(jnp.where(upper, total, 0.0), axis=(0, 1), keepdims=True)
            dual_all = jnp.sum(jnp.where(upper, 0.0, total), axis=(0, 1), keepdims=True)
            ratio = jnp.sqrt((dual_all + NORM_EPS) / (primal + NORM_EPS))
            return jnp.sqrt(ratio if weight is None else weight * ratio)

    weight = finish_norms(ITERS - 1, weight)
    weight_out[0] = jnp.sum(weight)
    for copy in sent:
        copy.wait_send()
    for it in range(ITERS):
        each_peer(lambda step: norm_copy(it, step).wait_send())
    for copy in outgoing:
        copy.wait()


def store_kernel(*refs):
    count = (len(refs) - 2) // 3
    sources, places, held = refs[:count], refs[count : 2 * count], refs[2 * count : 3 * count]
    in_sem, out_sem = refs[-2:]
    loads = [pltpu.make_async_copy(sources[i], held[i], in_sem.at[i]) for i in range(count)]
    stores = [pltpu.make_async_copy(held[i], places[i], out_sem.at[i]) for i in range(count)]
    for copy in loads:
        copy.start()
    for load, store in zip(loads, stores):
        load.wait()
        store.start()
    for copy in stores:
        copy.wait()


def on_device(
    segment_flow, linepack, mass_dual, momentum_dual, contract_dual, flow_cost, injection, contract_target,
    friction_table, friction_class, matching, contract_map,
):
    H, S, W = segment_flow.shape
    C = contract_dual.shape[3]
    R = contract_dual.shape[2]
    pipes, hours, segs = lax.axis_size("pipe"), lax.axis_size("hour"), lax.axis_size("seg")
    peers = pipes * hours * segs
    T = W * pipes
    f32, i32 = jnp.float32, jnp.int32
    anywhere = pl.BlockSpec(memory_space=pl.ANY)
    hbm = pl.BlockSpec(memory_space=pltpu.HBM)
    smem = pl.BlockSpec(memory_space=pltpu.SMEM)
    cells = jax.ShapeDtypeStruct((H, S, W), f32)
    turns = 2 * ITERS
    dma = pltpu.SemaphoreType.DMA
    outs = pl.pallas_call(
        functools.partial(kernel, (pipes, hours, segs, H, S, W, C, R, T)),
        out_shape=(cells,) * 4
        + (jax.ShapeDtypeStruct((H, R, C), f32), jax.ShapeDtypeStruct((1,), f32)),
        in_specs=[smem] + [hbm] * 11,
        out_specs=(anywhere,) * 5 + (smem,),
        scratch_shapes=[
            pltpu.VMEM((ITERS + 1, H, S, W), f32),
            pltpu.VMEM((ITERS + 1, H, S, W), f32),
            pltpu.VMEM((ITERS + 1, H, S, W), f32),
            pltpu.VMEM((ITERS + 1, H, S, W), f32),
            pltpu.VMEM((ITERS + 1, H, R, C), f32),
            pltpu.VMEM((H, S, W), f32),
            pltpu.VMEM((H, S, W), f32),
            pltpu.VMEM((H, R, C), f32),
            pltpu.VMEM((S, W), i32),
            pltpu.VMEM((1, T), i32),
            pltpu.VMEM((H, T), i32),
            pltpu.VMEM((S, W), f32),
            pltpu.VMEM((ITERS, H, S, W), f32),
            pltpu.VMEM((ITERS, H, S, W), f32),
            pltpu.VMEM((H, C, W), jnp.bfloat16),
            pltpu.VMEM((T, W), jnp.bfloat16),
            pltpu.VMEM((turns, 2 * H, W), f32),
            pltpu.VMEM((turns, pipes, 2 * H, W), f32),
            pltpu.VMEM((turns, S, W), f32),
            pltpu.VMEM((ITERS, pipes, H, R, C), f32),
            pltpu.VMEM((ITERS, pipes, H, R, C), f32),
            pltpu.VMEM((ITERS, pipes, H, R, C), f32),
            pltpu.VMEM((ITERS, 8, LANES), f32),
            pltpu.VMEM((ITERS, peers, 8, LANES), f32),
            dma((11,)),
            dma((5,)),
            dma((turns, pipes)),
            dma((turns, pipes)),
            dma((turns,)),
            dma((turns,)),
            dma((ITERS, pipes)),
            dma((ITERS, pipes)),
            dma((ITERS, pipes)),
            dma((ITERS, pipes)),
            dma((ITERS, peers)),
            dma((ITERS, peers)),
        ],
        compiler_params=pltpu.CompilerParams(
            collective_id=0, has_side_effects=True, vmem_limit_bytes=63 * 1024 * 1024
        ),
        cost_estimate=pl.CostEstimate(flops=10**8, bytes_accessed=2 * 10**6, transcendentals=0),
    )(
        friction_table, segment_flow, linepack, mass_dual, momentum_dual, contract_dual.reshape(H, R, C),
        flow_cost, injection, contract_target.reshape(H, R, C), friction_class, matching.reshape(1, T),
        contract_map,
    )
    stored = pl.pallas_call(
        store_kernel,
        out_shape=(cells,) * 4 + (jax.ShapeDtypeStruct((H, R, C), f32),),
        in_specs=[anywhere] * 5,
        out_specs=(hbm,) * 5,
        scratch_shapes=[pltpu.VMEM((H, S, W), f32)] * 4
        + [pltpu.VMEM((H, R, C), f32), dma((5,)), dma((5,))],
        compiler_params=pltpu.CompilerParams(vmem_limit_bytes=63 * 1024 * 1024),
    )(*outs[:5])
    return tuple(stored[:4]) + (stored[4].reshape(contract_dual.shape), outs[5])


def solution(mesh):
    cells = P(("groups", "hour"), "seg", "pipe")
    contracts = P(("groups", "hour"), "seg", "pipe", None)
    return jax.shard_map(
        on_device,
        mesh=mesh,
        in_specs=(
            cells, cells, cells, cells, contracts, cells, cells, contracts,
            P(), P("seg", ("groups", "pipe")), P("groups"), P(("groups", "hour"), None),
        ),
        out_specs=(cells, cells, cells, cells, contracts, P("groups")),
        check_vma=False,
    )
```
